128 devices in a mesh: seg: 32 (over x, z, core), head: 4 (over y).
Axes of the slice: x: 4, y: 4, z: 4, core: 2. Of those that a mesh axis runs over, the one named last changes fastest.
Arguments:
- token_ids: int32 [4096], P('seg'), may hold values from 0 to 31999
- embed_table: bfloat16 [32000, 2560], P('seg', 'head'), may hold values from -6 to 6
- norm_gains: float32 [2, 2560], replicated, may hold values from 0.1 to 1.9
- query_weight: bfloat16 [2, 2560, 2048], P(None, None, 'head')
- key_weight: bfloat16 [2, 2560, 2048], P(None, None, 'head')
- value_weight: bfloat16 [2, 2560, 2048], P(None, None, 'head'), may hold values from -0.125 to 0.125
- out_weight: bfloat16 [2, 2048, 2560], P(None, 'head'), may hold values from -0.125 to 0.125
Outputs:
- final_states: bfloat16 [4096, 2560], P(('seg', 'head'))
The draws below stay inside these ranges and needn't reach their ends.
Inputs may be any that keep to these rules, and one draw needn't show every extreme that they name: `token_ids`: token ids of the book span in reading order.
All inputs are finite; a program needn't handle non-finite values.
Results may differ from the reference program's by a relative error of at most 0.04.
Values may be sent and summed in bfloat16 or wider, within the bound.
A program may use at most 128 MiB of HBM per device.

```python
import math
import jax
import jax.numpy as jnp
import numpy as np
from jax import lax

D = 2560
HEADS = 32
HD = 64
VOCAB = 32000
LAYERS = 2
SEG = 128
TOKENS = 4096
N_SEG = 32


def spread_normal(key, factor):
    values = jax.random.normal(key, (LAYERS, D, HEADS * HD), jnp.float32)
    return (values * (factor / D ** 0.5)).astype(jnp.bfloat16)


def draw_query_weight(key, part):
    key = jax.random.fold_in(key, 11)
    return spread_normal(key, 1.0)


def draw_key_weight(key, part):
    key = jax.random.fold_in(key, 23)
    return spread_normal(key, 1.0)


def place_ends(array, key, smallest, high):
    extent = array.shape
    place = [jax.random.randint(jax.random.fold_in(key, axis), (), 0, extent[axis]) for axis in range(len(extent))]
    array = array.at[tuple(place)].set(smallest)
    longest = extent.index(max(extent))
    place[longest] = (place[longest] + 1) % extent[longest]
    return array.at[tuple(place)].set(high)


def levels(rng, shape, cuts, smallest, largest):
    def one(dim, blocks):
        draws = jax.random.uniform(jax.random.fold_in(jax.random.fold_in(rng, 6), dim), (blocks,), jnp.float32, smallest / len(cuts), largest / len(cuts))
        return jnp.repeat(jnp.exp(draws), shape[dim] // blocks).reshape((-1,) + (1,) * (len(shape) - dim - 1))

    factor_of = one(*cuts[0])
    for cut in cuts[1:]:
        factor_of = factor_of * one(*cut)
    return factor_of


def cumulative_ranks(amount, skew):
    portions = [(1 << 20) // math.isqrt(rank ** skew) + 1 for rank in range(1, amount + 1)]
    deviation = 1 + sum(portions) // (1 << 30)
    return np.cumsum(np.array([max(1, weight // deviation) for weight in portions]))


def ranked(stream_key, dims, number_of, skew):
    table = cumulative_ranks(number_of, skew)
    pick = jax.random.randint(jax.random.fold_in(stream_key, 1), dims, 0, int(table[number_of - 1]))
    standing = jnp.searchsorted(jnp.asarray(table, jnp.int32), pick, side="right")
    return jax.random.permutation(jax.random.fold_in(stream_key, 2), number_of)[standing].astype(jnp.int32)


def centred(key, extent, width, reach, split=(), kind=jnp.bfloat16):
    result = jax.random.normal(key, extent, jnp.float32) * width
    if len(split) > 0:
        result = levels(key, extent, split, -0.22, 0.18) * result
    return jnp.clip(result, min=-reach, max=reach).astype(kind)


def setup_inputs(seed: int = 0) -> dict:
    keys = jax.random.split(jax.random.key(seed), 8)
    return {
        "token_ids": place_ends(ranked(keys[0], (TOKENS,), VOCAB, 2), jax.random.fold_in(keys[0], 3), 0, VOCAB - 1).astype(jnp.int32),
        "embed_table": centred(keys[1], (VOCAB, D), 1.0, 6.0, ((0, 32), (1, 4))),
        "norm_gains": jnp.clip(1.0 + 0.18 * jax.random.normal(keys[2], (LAYERS, D), jnp.float32), 0.1, 1.9),
        "query_weight": draw_query_weight(jax.random.fold_in(keys[7], 71), 0),
        "key_weight": draw_key_weight(jax.random.fold_in(keys[7], 71), 0),
        "value_weight": centred(keys[5], (LAYERS, D, HEADS * HD), D ** -0.5, 0.125, ((2, 4),)),
        "out_weight": centred(keys[6], (LAYERS, HEADS * HD, D), (HEADS * HD) ** -0.5, 0.125, ((1, 4),)),
    }


EPSILON = 1e-05

def rotate(field, positions):
    half_dim = field.shape[-1] // 2
    frequency = 10000.0 ** (-jnp.arange(half_dim, dtype=jnp.float32) / half_dim)
    angles = positions.astype(jnp.float32)[:, None] * frequency[None, :]
    cosine = jnp.cos(angles)[:, None, :]
    sine = jnp.sin(angles)[:, None, :]
    front = field[..., :half_dim]
    back = field[..., half_dim:]
    return jnp.concatenate([front * cosine - back * sine, front * sine + back * cosine], axis=-1)

def normalize(states, gain):
    widened = states.astype(jnp.float32)
    mean_square = lax.optimization_barrier(jnp.mean(widened * widened, axis=-1, keepdims=True))
    return (widened * lax.rsqrt(mean_square + EPSILON) * gain).astype(jnp.bfloat16)

def attend_block(queries, keys_all, values_all, has_memory):
    count = queries.shape[0]
    scores = jnp.einsum('qhd,khd->hqk', queries.astype(jnp.float32), keys_all.astype(jnp.float32)) * queries.shape[-1] ** (-0.5)
    query_place = jnp.arange(count, dtype=jnp.int32)[:, None]
    key_place = jnp.arange(2 * count, dtype=jnp.int32)[None, :]
    allowed = jnp.where(key_place < count, has_memory, key_place - count <= query_place)
    scores = jnp.where(allowed[None], scores, -1e+30)
    top_score = lax.optimization_barrier(jnp.max(scores, axis=-1, keepdims=True))
    weights = jnp.exp(scores - top_score)
    probs = (weights / lax.optimization_barrier(jnp.sum(weights, axis=-1, keepdims=True))).astype(jnp.bfloat16)
    mixed = jnp.einsum('hqk,khd->qhd', probs.astype(jnp.float32), values_all.astype(jnp.float32))
    return mixed.astype(jnp.bfloat16).reshape(count, -1)

def reference(token_ids, embed_table, norm_gains, query_weight, key_weight, value_weight, out_weight):
    states = embed_table[token_ids]
    positions = jnp.arange(TOKENS, dtype=jnp.int32)
    for depth in range(LAYERS):
        normed = normalize(states, norm_gains[depth])
        queries = rotate(jnp.dot(normed, query_weight[depth], preferred_element_type=jnp.float32).reshape(TOKENS, HEADS, HD), positions).astype(jnp.bfloat16)
        keys_book = rotate(jnp.dot(normed, key_weight[depth], preferred_element_type=jnp.float32).reshape(TOKENS, HEADS, HD), positions).astype(jnp.bfloat16)
        values_book = jnp.dot(normed, value_weight[depth], preferred_element_type=jnp.float32).astype(jnp.bfloat16).reshape(TOKENS, HEADS, HD)

        def per_segment(segment, queries=queries, keys_book=keys_book, values_book=values_book):
            start = (segment * SEG).astype(jnp.int32)
            before = (jnp.maximum(segment - 1, 0) * SEG).astype(jnp.int32)
            query_block = lax.dynamic_slice_in_dim(queries, start, SEG, 0)
            key_block = jnp.concatenate([lax.dynamic_slice_in_dim(keys_book, before, SEG, 0), lax.dynamic_slice_in_dim(keys_book, start, SEG, 0)], 0)
            value_block = jnp.concatenate([lax.dynamic_slice_in_dim(values_book, before, SEG, 0), lax.dynamic_slice_in_dim(values_book, start, SEG, 0)], 0)
            return attend_block(query_block, key_block, value_block, segment > 0)
        mixed = lax.map(per_segment, jnp.arange(N_SEG, dtype=jnp.int32)).reshape(TOKENS, HEADS * HD)
        states = (states.astype(jnp.float32) + jnp.dot(mixed, out_weight[depth], preferred_element_type=jnp.float32)).astype(jnp.bfloat16)
    return states
```

```python
import functools

import jax
import jax.numpy as jnp
import numpy as np
from jax import lax
from jax.experimental import pallas as pl
from jax.experimental.pallas import tpu as pltpu
from jax.sharding import PartitionSpec as P

HD = 64
LAYERS = 2
EPSILON = 1e-05
SLOTS = 32
MESH = pl.DeviceIdType.MESH
F32 = jnp.float32
BF16 = jnp.bfloat16
I32 = jnp.int32


def shifted(value, axis, steps):
    count = lax.axis_size(axis)
    leading, last = (max(0, -steps), min(count, count - steps))
    return lax.ppermute(value, axis, [(source, source + steps) for source in range(leading, last)])


def rotate(field, positions):
    half_dim = field.shape[-1] // 2
    frequency = 10000.0 ** (-jnp.arange(half_dim, dtype=jnp.float32) / half_dim)
    angles = positions.astype(jnp.float32)[:, None] * frequency[None, :]
    cosine = jnp.cos(angles)[:, None, :]
    sine = jnp.sin(angles)[:, None, :]
    front = field[..., :half_dim]
    back = field[..., half_dim:]
    return jnp.concatenate([front * cosine - back * sine, front * sine + back * cosine], axis=-1)


def normalize(states, gain):
    widened = states.astype(jnp.float32)
    mean_square = jnp.mean(widened * widened, axis=-1, keepdims=True)
    return (widened * lax.rsqrt(mean_square + EPSILON) * gain).astype(jnp.bfloat16)


def attend_block(queries, keys_all, values_all, has_memory):
    count = queries.shape[0]
    scores = jnp.einsum(
        "qhd,khd->hqk", queries, keys_all, preferred_element_type=jnp.float32
    ) * queries.shape[-1] ** (-0.5)
    query_place = jnp.arange(count, dtype=jnp.int32)[:, None]
    key_place = jnp.arange(2 * count, dtype=jnp.int32)[None, :]
    allowed = jnp.where(key_place < count, has_memory, key_place - count <= query_place)
    scores = jnp.where(allowed[None], scores, -1e30)
    top_score = jnp.max(scores, axis=-1, keepdims=True)
    weights = jnp.exp(scores - top_score)
    probs = (weights / jnp.sum(weights, axis=-1, keepdims=True)).astype(jnp.bfloat16)
    mixed = jnp.einsum("hqk,khd->qhd", probs, values_all, preferred_element_type=jnp.float32)
    return mixed.astype(jnp.bfloat16).reshape(count, -1)


def general(token_ids, embed_table, norm_gains, query_weight, key_weight, value_weight, out_weight):
    seg_len = token_ids.shape[0]
    head_count = lax.axis_size("head")
    local_heads = query_weight.shape[2] // HD
    book_ids = lax.all_gather(token_ids, "seg", axis=0, tiled=True)
    vocab_rows = embed_table.shape[0]
    seg_index = lax.axis_index("seg")
    vocab_start = seg_index * vocab_rows
    chosen = book_ids - vocab_start
    inside = ((chosen >= 0) & (chosen < vocab_rows)).astype(jnp.float32)
    clamped = jnp.clip(chosen, 0, vocab_rows - 1)
    rows = jnp.take(embed_table, clamped, axis=0).astype(jnp.float32)
    embedded = lax.psum_scatter(
        (rows * inside[:, None]).astype(jnp.bfloat16), "seg", scatter_dimension=0, tiled=True
    )
    states = lax.all_gather(embedded, "head", axis=1, tiled=True)
    positions = seg_index * seg_len + jnp.arange(seg_len, dtype=jnp.int32)
    has_memory = seg_index > 0
    row_count = seg_len // head_count
    row_start = lax.axis_index("head") * row_count

    def project(normed, weight, depth):
        return jnp.dot(normed, weight[depth], preferred_element_type=jnp.float32).reshape(
            seg_len, local_heads, HD
        )

    normed = normalize(states, norm_gains[0])
    residual = states
    for depth in range(LAYERS):
        queries = rotate(project(normed, query_weight, depth), positions).astype(jnp.bfloat16)
        keys_now = rotate(project(normed, key_weight, depth), positions).astype(jnp.bfloat16)
        values_now = project(normed, value_weight, depth).astype(jnp.bfloat16)
        normed_past = shifted(normed, "seg", 1)
        keys_past = rotate(project(normed_past, key_weight, depth), positions - seg_len).astype(
            jnp.bfloat16
        )
        values_past = project(normed_past, value_weight, depth).astype(jnp.bfloat16)
        keys_all = jnp.concatenate([keys_past, keys_now], 0)
        values_all = jnp.concatenate([values_past, values_now], 0)
        mixed = attend_block(queries, keys_all, values_all, has_memory)
        summed = lax.psum(
            jnp.dot(mixed, out_weight[depth], preferred_element_type=jnp.float32), "head"
        )
        residual = (residual.astype(jnp.float32) + summed).astype(jnp.bfloat16)
        if depth + 1 < LAYERS:
            normed = normalize(residual, norm_gains[depth + 1])
    return lax.dynamic_slice_in_dim(residual, row_start, row_count, 0)


def dot(a, b):
    return jnp.dot(a, b, preferred_element_type=F32)


def dot_nt(a, b):
    return lax.dot_general(a, b, (((1,), (1,)), ((), ())), preferred_element_type=F32)


def kernel(
    n_seg, vr, t_len, cw, hw,
    ids_hbm, tab_hbm, gain_hbm, wq_hbm, wk_hbm, wv_hbm, wo_hbm, rope_t_hbm, rope_s_hbm,
    out_ref, flag_ref,
    ids_v, gain_v, rope_t, rope_s, tab, wq, wk, wv, wo,
    req_send, req_recv, flag_send, flag_recv, pk_send, pk_recv,
    st, acc, kv_own, kv_past, q_own, o_part, mx_part, mixed,
    part0, part1, frecv0, frecv1, comb0, comb1, rrecv0, rrecv1,
    l_sem, w_sem, tab_sem, req_sem, flag_sem, pk_sem,
    ag_s, ag_r, agf_s, agf_r, kv_s, kv_r, rs_s, rs_r,
):
    s = lax.axis_index("seg")
    h = lax.axis_index("head")
    chip, core = s // 2, lax.rem(s, 2)
    n_chip = n_seg // 2
    up, dn, opp = lax.rem(h + 1, 4), lax.rem(h + 3, 4), lax.rem(h + 2, 4)
    sib = s + 1 - 2 * core
    nxt, prv = lax.rem(s + 1, n_seg), lax.rem(s + n_seg - 1, n_seg)
    blocks = (h, dn, up, opp)

    def remote(src, dst, ss, rs, seg, head):
        return pltpu.make_async_remote_copy(
            src_ref=src, dst_ref=dst, send_sem=ss, recv_sem=rs,
            device_id=(seg, head), device_id_type=MESH,
        )

    bar = pltpu.get_barrier_semaphore()

    def hello(seg, head):
        pl.semaphore_signal(bar, inc=1, device_id=(seg, head), device_id_type=MESH)

    for other in (up, dn, opp):
        hello(s, other)
    hello(nxt, h)
    hello(prv, h)

    def hello_chip(k, c):
        hello(2 * lax.rem(chip + k, n_chip) + core, h)
        return c

    lax.fori_loop(1, n_chip, hello_chip, 0)

    loads = [
        pltpu.make_async_copy(a, b, l_sem.at[i])
        for i, (a, b) in enumerate(
            [(ids_hbm, ids_v), (tab_hbm, tab.at[core]), (gain_hbm, gain_v),
             (rope_t_hbm, rope_t), (rope_s_hbm, rope_s)]
        )
    ]
    for c in loads:
        c.start()
    weights = {}
    for layer in range(LAYERS):
        for i, (a, b) in enumerate([(wk_hbm, wk), (wv_hbm, wv), (wq_hbm, wq), (wo_hbm, wo)]):
            c = pltpu.make_async_copy(a.at[layer], b.at[layer], w_sem.at[layer, i])
            c.start()
            weights[layer, i] = c

    loads[0].wait()
    sub = lax.broadcasted_iota(I32, (t_len, t_len), 0)
    lane = lax.broadcasted_iota(I32, (t_len, t_len), 1)
    idr = jnp.broadcast_to(ids_v[...], (t_len, t_len))
    idc = idr.T

    def chip_of(ids):
        return ((ids.astype(F32) + 0.5) * (1.0 / (2 * vr))).astype(I32)

    pr, pc = chip_of(idr), chip_of(idc)
    same = idr == idc
    one = jnp.ones((), I32)
    zero = jnp.zeros((), I32)
    dup_row = jnp.sum(jnp.where(same & (sub < lane), one, zero), axis=0, keepdims=True)
    dup_col = jnp.sum(jnp.where(same & (lane < sub), one, zero), axis=1, keepdims=True)
    first_row, first_col = dup_row == 0, dup_col == 0
    peer = pr == pc
    rank_row = jnp.sum(jnp.where(peer & (idc < idr) & first_col, one, zero), axis=0, keepdims=True)
    rank_col = jnp.sum(jnp.where(peer & (idr < idc) & first_row, one, zero), axis=1, keepdims=True)
    full = jnp.where(jnp.max(rank_row, axis=1, keepdims=True) >= SLOTS, one, zero)
    pcol = pc[:, 0:1]
    wanted = jnp.broadcast_to(jnp.where(first_col, pcol * t_len + rank_col, -1), (t_len, t_len))
    local_id = idc - 2 * vr * pc + 1
    slot_key = pcol * SLOTS + rank_col
    lane_row = lane[0:1]

    def make_request(p, c):
        row = jnp.sum(jnp.where(wanted == p * t_len + lane, local_id, zero), axis=0, keepdims=True) - 1
        req_send[p] = jnp.where(lane_row == t_len - 1, full, row)
        return c

    lax.fori_loop(0, n_chip, make_request, 0)
    req_recv[chip] = req_send[chip]

    pl.semaphore_wait(bar, 3 + 2 + n_chip - 1)

    def send_request(k, c):
        p = lax.rem(chip + k, n_chip)
        remote(req_send.at[p], req_recv.at[chip], req_sem.at[0], req_sem.at[1], 2 * p + core, h).start()
        return c

    lax.fori_loop(1, n_chip, send_request, 0)
    tab_copy = remote(tab_hbm, tab.at[core], tab_sem.at[0], tab_sem.at[1], sib, h)
    tab_copy.start()
    loads[1].wait()
    others = req_recv.at[pl.ds(0, n_chip - 1)]
    pltpu.make_async_copy(others, others, req_sem.at[1]).wait()

    reqs = jnp.concatenate([req_recv[p] for p in range(n_chip)], axis=0)
    any_full = jnp.max(reqs, axis=0, keepdims=True)
    any_full = jnp.max(jnp.where(lane_row == t_len - 1, any_full, zero), axis=1, keepdims=True)
    any_full = jnp.broadcast_to(any_full, (8, t_len))
    flag_send[...] = any_full
    flag_copy = remote(flag_send, flag_recv, flag_sem.at[0], flag_sem.at[1], sib, h)
    flag_copy.start()

    if n_chip < t_len:
        reqs = jnp.concatenate([reqs, jnp.zeros((t_len - n_chip, t_len), I32)], axis=0)
    reqs_t = reqs.T
    group = min(4, n_chip)
    row_iota = lax.broadcasted_iota(I32, (SLOTS, vr), 1)
    hot = [
        jnp.concatenate(
            [jnp.broadcast_to(reqs_t[:SLOTS, g + i:g + i + 1], (SLOTS, vr)) - row_iota for i in range(group)],
            axis=0,
        )
        for g in range(0, n_chip, group)
    ]
    tab_copy.wait_recv()
    for gi, g in enumerate(range(0, n_chip, group)):
        lo = jnp.where(hot[gi] == 0, 1.0, 0.0).astype(BF16)
        hi = jnp.where(hot[gi] == vr, 1.0, 0.0).astype(BF16)
        rows = (dot(lo, tab[0]) + dot(hi, tab[1])).astype(BF16)
        for i in range(group):
            pk_send[g + i] = rows[i * SLOTS:(i + 1) * SLOTS]

    pk_recv[chip] = pk_send[chip]

    def send_rows(k, c):
        p = lax.rem(chip + k, n_chip)
        remote(pk_send.at[p], pk_recv.at[chip], pk_sem.at[0], pk_sem.at[1], 2 * p + core, h).start()
        return c

    lax.fori_loop(1, n_chip, send_rows, 0)

    for c in loads[2:]:
        c.wait()
    cos_t, sin_t = rope_t[0], rope_t[1]
    cos_s, sin_s = rope_s[0, pl.ds(s, 1), :], rope_s[1, pl.ds(s, 1), :]
    cosine = cos_t * cos_s - sin_t * sin_s
    sine = sin_t * cos_s + cos_t * sin_s
    lane128 = lax.broadcasted_iota(I32, (t_len, 128), 1)
    front = lax.rem(lane128, HD) < HD // 2
    sine = jnp.where(front, -sine, sine)

    def rope(x, scale):
        pieces = []
        for j in range(0, hw, 128):
            y = x[:, j:j + 128] * scale
            partner = jnp.where(front, pltpu.roll(y, 128 - HD // 2, 1), pltpu.roll(y, HD // 2, 1))
            pieces.append(y * cosine + partner * sine)
        return jnp.concatenate(pieces, axis=1)

    slots_iota = lax.broadcasted_iota(I32, (t_len, n_chip * SLOTS), 1)
    unpack = jnp.where(jnp.broadcast_to(slot_key, slots_iota.shape) == slots_iota, 1.0, 0.0).astype(BF16)

    others = pk_recv.at[pl.ds(0, n_chip - 1)]
    pltpu.make_async_copy(others, others, pk_sem.at[1]).wait()
    packed = pk_recv[...].reshape(n_chip * SLOTS, cw)
    st[0, 0] = dot(unpack, packed).astype(BF16)

    causal = lane[:, :t_len] <= sub[:, :t_len]
    causal2 = jnp.concatenate([causal, causal], axis=0)
    head_a = lane128 < HD
    ones = jnp.ones((t_len, 128), BF16)
    half_t = t_len // 2
    sends = []

    for layer in range(LAYERS):
        quarter = t_len // 4
        ups, dns, fws = [], [], []
        for c in range(4):
            a = pl.ds(c * quarter, quarter)
            e = 3 - c
            b = pl.ds(e * quarter, quarter)
            cu = remote(st.at[layer, 0, a], st.at[layer, 1, a], ag_s.at[layer, 0, c], ag_r.at[layer, 0, c], s, up)
            cd = remote(st.at[layer, 0, b], st.at[layer, 2, b], ag_s.at[layer, 1, e], ag_r.at[layer, 1, e], s, dn)
            cu.start()
            cd.start()
            ups.append(cu)
            dns.append(cd)

        def project(k, first):
            x = st[layer, k].astype(F32)
            rows = pl.ds(pl.multiple_of(blocks[k] * cw, cw), cw)
            cols = pl.ds(pl.multiple_of(blocks[k] * cw, 128), cw)
            gain = gain_v[pl.ds(layer, 1), cols]
            xg = (x * gain).astype(BF16)
            for i, w in enumerate((wk, wv, wq)):
                y = dot(xg, w[layer, rows, :])
                if first:
                    acc[i] = y
                else:
                    acc[i] += y
            return jnp.sum(x * x, axis=1, keepdims=True)

        for i in range(3):
            weights[layer, i].wait()
        square = project(0, True)
        for c in range(2):
            a = pl.ds(c * quarter, quarter)
            e = 3 - c
            b = pl.ds(e * quarter, quarter)
            ups[c].wait_recv()
            fu = remote(st.at[layer, 1, a], st.at[layer, 3, a], agf_s.at[layer, c], agf_r.at[layer, c], s, up)
            fu.start()
            dns[c].wait_recv()
            fd = remote(st.at[layer, 2, b], st.at[layer, 3, b], agf_s.at[layer, e], agf_r.at[layer, e], s, dn)
            fd.start()
            fws += [fu, fd]
        for c in range(2, 4):
            ups[c].wait_recv()
        square += project(1, False)
        for c in range(2, 4):
            dns[c].wait_recv()
        square += project(2, False)
        for f in fws:
            f.wait_recv()
        square += project(3, False)
        sends += ups + dns + fws
        scale = lax.rsqrt(square * (1.0 / (4 * cw)) + EPSILON)

        kv_own[layer, 0] = rope(acc[0], scale).astype(BF16)
        k_copy = remote(kv_own.at[layer, 0], kv_past.at[layer, 0], kv_s.at[layer, 0], kv_r.at[layer, 0], nxt, h)
        k_copy.start()
        kv_own[layer, 1] = (acc[1] * scale).astype(BF16)
        v_copy = remote(kv_own.at[layer, 1], kv_past.at[layer, 1], kv_s.at[layer, 1], kv_r.at[layer, 1], nxt, h)
        v_copy.start()
        sends += [k_copy, v_copy]
        q_own[...] = (rope(acc[2], scale) * HD ** (-0.5)).astype(BF16)

        def queries_of(j):
            q = q_own[:, j:j + 128]
            none = jnp.zeros_like(q)
            return jnp.concatenate([jnp.where(head_a, q, none), jnp.where(head_a, none, q)], axis=0)

        for i, j in enumerate(range(0, hw, 128)):
            scores = dot_nt(queries_of(j), kv_own[layer, 0, :, j:j + 128])
            scores = jnp.where(causal2, scores, -1e30)
            top = jnp.max(scores, axis=1, keepdims=True)
            e = jnp.exp(scores - top).astype(BF16)
            values = jnp.concatenate([kv_own[layer, 1, :, j:j + 128], ones], axis=1)
            o_part[i] = dot(e, values)
            mx_part[i] = jnp.broadcast_to(top, (2 * t_len, 128))
        k_copy.wait_recv()
        v_copy.wait_recv()
        for i, j in enumerate(range(0, hw, 128)):
            scores = dot_nt(queries_of(j), kv_past[layer, 0, :, j:j + 128])
            scores = jnp.where(s > 0, scores, -1e30)
            old = mx_part[i]
            top = jnp.maximum(old, jnp.max(scores, axis=1, keepdims=True))
            e = jnp.exp(scores - top).astype(BF16)
            keep = jnp.exp(old - top)
            values = jnp.concatenate([kv_past[layer, 1, :, j:j + 128], ones], axis=1)
            o = dot(e, values)
            num = o_part[i, :, :128] * keep + o[:, :128]
            den = o_part[i, :, 128:] * keep + o[:, 128:]
            m = num / den
            mixed[:, j:j + 128] = jnp.where(head_a, m[:t_len], m[t_len:]).astype(BF16)

        weights[layer, 3].wait()
        last = layer == LAYERS - 1
        part, comb, frecv, rrecv = (
            (part1, comb1, frecv1, rrecv1) if last else (part0, comb0, frecv0, rrecv0)
        )
        n_row = part.shape[1]
        lo, hi = pl.ds(0, n_row // 2), pl.ds(n_row // 2, n_row // 2)

        def send(i, src, dst, to):
            c = remote(src, dst, rs_s.at[layer, i], rs_r.at[layer, i], s, to)
            c.start()
            sends.append(c)
            return c

        def far():
            return [
                send(0, part.at[opp, lo], frecv.at[0], up),
                send(1, part.at[opp, hi], frecv.at[1], dn),
            ]

        if last:
            for b in range(4):
                y = dot(mixed[...], wo[layer, :, b * cw:(b + 1) * cw]).astype(BF16)
                for d in range(4):
                    part[d, :, b * cw:(b + 1) * cw] = y[d * n_row:(d + 1) * n_row]
            f = far()
        else:
            for b in (opp, up, dn, h):
                y = dot(mixed[...], wo[layer, :, pl.ds(pl.multiple_of(b * cw, 128), cw)])
                part[b] = y.astype(BF16)
                if b is opp:
                    f = far()
        r = [
            send(2, part.at[up, hi], rrecv.at[0, hi], up),
            send(3, part.at[dn, lo], rrecv.at[1, lo], dn),
        ]
        f[0].wait_recv()
        comb[0] = (part[up, lo].astype(F32) + frecv[0].astype(F32)).astype(BF16)
        r.append(send(4, comb.at[0], rrecv.at[0, lo], up))
        f[1].wait_recv()
        comb[1] = (part[dn, hi].astype(F32) + frecv[1].astype(F32)).astype(BF16)
        r.append(send(5, comb.at[1], rrecv.at[1, hi], dn))
        for c in r:
            c.wait_recv()
        total = part[h].astype(F32) + rrecv[0].astype(F32) + rrecv[1].astype(F32)
        if last:
            for k in range(4):
                cols = pl.ds(pl.multiple_of(blocks[k] * cw, 128), cw)
                rows = pl.ds(pl.multiple_of(h * n_row, n_row), n_row)
                out_ref[:, cols] = st[layer, k, rows, :].astype(F32)
            out_ref[...] += total
        else:
            st[layer + 1, 0] = (st[layer, 0].astype(F32) + total).astype(BF16)

    flag_copy.wait()
    flag_ref[...] = jnp.maximum(flag_send[...], flag_recv[...])
    tab_copy.wait_send()
    others = req_send.at[pl.ds(0, n_chip - 1)]
    pltpu.make_async_copy(others, others, req_sem.at[0]).wait()
    others = pk_send.at[pl.ds(0, n_chip - 1)]
    pltpu.make_async_copy(others, others, pk_sem.at[0]).wait()
    for c in sends:
        c.wait_send()


def rotary_tables(n_seg, t_len):
    freq = 10000.0 ** (-np.arange(HD // 2, dtype=np.float64) / (HD // 2))
    freq = np.tile(freq, 128 // (HD // 2))[None]
    local = np.arange(t_len, dtype=np.float64)[:, None] * freq
    start = (np.arange(n_seg, dtype=np.float64) * t_len)[:, None] * freq
    both = lambda a: np.stack([np.cos(a), np.sin(a)]).astype(np.float32)
    return both(local), both(start)


def body(n_seg, token_ids, embed_table, norm_gains, query_weight, key_weight, value_weight, out_weight):
    t_len = token_ids.shape[0]
    vr, cw = embed_table.shape
    hw = query_weight.shape[2]
    n_chip = n_seg // 2
    rope_t, rope_s = rotary_tables(n_seg, t_len)
    rows = t_len // 4
    vmem = pltpu.VMEM
    dma = pltpu.SemaphoreType.DMA
    any_spec = pl.BlockSpec(memory_space=pl.ANY)
    vmem_spec = pl.BlockSpec(memory_space=pltpu.VMEM)
    out, flag = pl.pallas_call(
        functools.partial(kernel, n_seg, vr, t_len, cw, hw),
        out_shape=(
            jax.ShapeDtypeStruct((rows, 4 * cw), F32),
            jax.ShapeDtypeStruct((8, t_len), I32),
        ),
        in_specs=[any_spec] * 9,
        out_specs=(vmem_spec, vmem_spec),
        scratch_shapes=[
            vmem((1, t_len), I32),
            vmem(norm_gains.shape, F32),
            vmem(rope_t.shape, F32),
            vmem(rope_s.shape, F32),
            vmem((2, vr, cw), BF16),
            vmem(query_weight.shape, BF16),
            vmem(key_weight.shape, BF16),
            vmem(value_weight.shape, BF16),
            vmem(out_weight.shape, BF16),
            vmem((n_chip, 1, t_len), I32),
            vmem((n_chip, 1, t_len), I32),
            vmem((8, t_len), I32),
            vmem((8, t_len), I32),
            vmem((n_chip, SLOTS, cw), BF16),
            vmem((n_chip, SLOTS, cw), BF16),
            vmem((LAYERS, 4, t_len, cw), BF16),
            vmem((3, t_len, hw), F32),
            vmem((LAYERS, 2, t_len, hw), BF16),
            vmem((LAYERS, 2, t_len, hw), BF16),
            vmem((t_len, hw), BF16),
            vmem((hw // 128, 2 * t_len, 256), F32),
            vmem((hw // 128, 2 * t_len, 128), F32),
            vmem((t_len, hw), BF16),
            vmem((4, t_len, cw), BF16),
            vmem((4, rows, 4 * cw), BF16),
            vmem((2, t_len // 2, cw), BF16),
            vmem((2, rows // 2, 4 * cw), BF16),
            vmem((2, t_len // 2, cw), BF16),
            vmem((2, rows // 2, 4 * cw), BF16),
            vmem((2, t_len, cw), BF16),
            vmem((2, rows, 4 * cw), BF16),
            dma((5,)),
            dma((LAYERS, 4)),
            dma((2,)),
            dma((2,)),
            dma((2,)),
            dma((2,)),
            dma((LAYERS, 2, 4)),
            dma((LAYERS, 2, 4)),
            dma((LAYERS, 4)),
            dma((LAYERS, 4)),
            dma((LAYERS, 2)),
            dma((LAYERS, 2)),
            dma((LAYERS, 6)),
            dma((LAYERS, 6)),
        ],
        compiler_params=pltpu.CompilerParams(
            collective_id=0, has_side_effects=True, vmem_limit_bytes=56 * 2 ** 20
        ),
        name="decoder",
    )(
        token_ids.reshape(1, t_len), embed_table, norm_gains,
        query_weight, key_weight, value_weight, out_weight,
        jnp.asarray(rope_t), jnp.asarray(rope_s),
    )
    return lax.cond(
        flag[0, 0] > 0,
        lambda: general(
            token_ids, embed_table, norm_gains, query_weight, key_weight, value_weight, out_weight
        ),
        lambda: out.astype(BF16),
    )


def solution(mesh):
    placed = (
        P("seg"),
        P("seg", "head"),
        P(),
        P(None, None, "head"),
        P(None, None, "head"),
        P(None, None, "head"),
        P(None, "head", None),
    )
    return jax.shard_map(
        functools.partial(body, mesh.shape["seg"]),
        mesh=mesh, in_specs=placed, out_specs=P(("seg", "head"), None), check_vma=False,
    )
```

```python
import functools

import jax
import jax.numpy as jnp
import numpy as np
from jax import lax
from jax.experimental import pallas as pl
from jax.experimental.pallas import tpu as pltpu
from jax.sharding import PartitionSpec as P

HD = 64
LAYERS = 2
EPSILON = 1e-05
SLOTS, ALL_SLOTS = 32, 128
MESH = pl.DeviceIdType.MESH
F32 = jnp.float32
BF16 = jnp.bfloat16
I32 = jnp.int32


def dot(a, b):
    return jnp.dot(a, b, preferred_element_type=F32)


def dot_nt(a, b):
    return lax.dot_general(a, b, (((1,), (1,)), ((), ())), preferred_element_type=F32)


def kernel(
    slots, n_seg, vr, t_len, cw, hw,
    ids_hbm, tab_hbm, gain_hbm, wq_hbm, wk_hbm, wv_hbm, wo_hbm, rope_t_hbm, rope_s_hbm,
    out_ref, flag_ref,
    ids_v, gain_v, rope_t, rope_s, tab, wq, wk, wv, wo,
    req_send, req_recv, flag_send, flag_recv, pk_send, pk_recv,
    st, acc, kv_own, kv_past, q_own, o_part, mx_part, mixed,
    part0, part1, frecv0, frecv1, comb0, comb1, rrecv0, rrecv1,
    l_sem, w_sem, tab_sem, req_sem, flag_sem, pk_sem,
    ag_s, ag_r, agf_s, agf_r, kv_s, kv_r, rs_s, rs_r,
):
    s = lax.axis_index("seg")
    h = lax.axis_index("head")
    chip, core = s // 2, lax.rem(s, 2)
    n_chip = n_seg // 2
    up, dn, opp = lax.rem(h + 1, 4), lax.rem(h + 3, 4), lax.rem(h + 2, 4)
    sib = s + 1 - 2 * core
    nxt, prv = lax.rem(s + 1, n_seg), lax.rem(s + n_seg - 1, n_seg)
    blocks = (h, dn, up, opp)

    def remote(src, dst, ss, rs, seg, head):
        return pltpu.make_async_remote_copy(
            src_ref=src, dst_ref=dst, send_sem=ss, recv_sem=rs,
            device_id=(seg, head), device_id_type=MESH,
        )

    bar = pltpu.get_barrier_semaphore()

    def hello(seg, head):
        pl.semaphore_signal(bar, inc=1, device_id=(seg, head), device_id_type=MESH)

    for other in (up, dn):
        hello(s, other)
    hello(sib, h)
    hello(prv, h)

    def hello_chip(k, c):
        hello(2 * lax.rem(chip + k, n_chip) + core, h)
        return c

    lax.fori_loop(1, n_chip, hello_chip, 0)

    loads = [
        pltpu.make_async_copy(a, b, l_sem.at[i])
        for i, (a, b) in enumerate(
            [(ids_hbm, ids_v), (tab_hbm, tab.at[core]), (gain_hbm, gain_v),
             (rope_t_hbm, rope_t), (rope_s_hbm, rope_s)]
        )
    ]
    for c in loads:
        c.start()
    weights = {}
    for layer in range(LAYERS):
        for i, (a, b) in enumerate([(wk_hbm, wk), (wv_hbm, wv), (wq_hbm, wq), (wo_hbm, wo)]):
            c = pltpu.make_async_copy(a.at[layer], b.at[layer], w_sem.at[layer, i])
            c.start()
            weights[layer, i] = c

    loads[0].wait()
    sub = lax.broadcasted_iota(I32, (t_len, t_len), 0)
    lane = lax.broadcasted_iota(I32, (t_len, t_len), 1)
    idr = jnp.broadcast_to(ids_v[...], (t_len, t_len))
    idc = idr.T

    def chip_of(ids):
        return ((ids.astype(F32) + 0.5) * (1.0 / (2 * vr))).astype(I32)

    pr, pc = chip_of(idr), chip_of(idc)
    same = idr == idc
    one = jnp.ones((), I32)
    zero = jnp.zeros((), I32)
    dup_row = jnp.sum(jnp.where(same & (sub < lane), one, zero), axis=0, keepdims=True)
    dup_col = jnp.sum(jnp.where(same & (lane < sub), one, zero), axis=1, keepdims=True)
    first_row, first_col = dup_row == 0, dup_col == 0
    peer = pr == pc
    rank_row = jnp.sum(jnp.where(peer & (idc < idr) & first_col, one, zero), axis=0, keepdims=True)
    rank_col = jnp.sum(jnp.where(peer & (idr < idc) & first_row, one, zero), axis=1, keepdims=True)
    full = jnp.where(jnp.max(rank_row, axis=1, keepdims=True) >= slots, one, zero)
    pcol = pc[:, 0:1]
    wanted = jnp.broadcast_to(jnp.where(first_col, pcol * t_len + rank_col, -1), (t_len, t_len))
    local_id = idc - 2 * vr * pc + 1
    slot_key = pcol * slots + rank_col
    lane_row = lane[0:1]

    def make_request(p, c):
        row = jnp.sum(jnp.where(wanted == p * t_len + lane, local_id, zero), axis=0, keepdims=True) - 1
        req_send[p] = jnp.where(lane_row == t_len - 1, full, row) if slots < t_len else row
        return c

    lax.fori_loop(0, n_chip, make_request, 0)
    req_recv[chip] = req_send[chip]

    pl.semaphore_wait(bar, 2 + 2 + n_chip - 1)

    def send_request(k, c):
        p = lax.rem(chip + k, n_chip)
        remote(req_send.at[p], req_recv.at[chip], req_sem.at[0], req_sem.at[1], 2 * p + core, h).start()
        return c

    lax.fori_loop(1, n_chip, send_request, 0)
    tab_copy = remote(tab_hbm, tab.at[core], tab_sem.at[0], tab_sem.at[1], sib, h)
    tab_copy.start()
    loads[1].wait()
    others = req_recv.at[pl.ds(0, n_chip - 1)]
    pltpu.make_async_copy(others, others, req_sem.at[1]).wait()

    reqs = jnp.concatenate([req_recv[p] for p in range(n_chip)], axis=0)
    any_full = jnp.max(reqs, axis=0, keepdims=True)
    any_full = jnp.max(jnp.where(lane_row == t_len - 1, any_full, zero), axis=1, keepdims=True)
    flag_send[...] = jnp.broadcast_to(any_full, (8, t_len))
    flag_copy = remote(flag_send, flag_recv, flag_sem.at[0], flag_sem.at[1], sib, h)
    flag_copy.start()

    if n_chip < t_len:
        reqs = jnp.concatenate([reqs, jnp.zeros((t_len - n_chip, t_len), I32)], axis=0)
    reqs_t = reqs.T
    group = min(t_len // slots, n_chip)
    row_iota = lax.broadcasted_iota(I32, (slots, vr), 1)
    hot = [
        jnp.concatenate(
            [jnp.broadcast_to(reqs_t[:slots, g + i:g + i + 1], (slots, vr)) - row_iota for i in range(group)],
            axis=0,
        )
        for g in range(0, n_chip, group)
    ]
    tab_copy.wait_recv()
    for gi, g in enumerate(range(0, n_chip, group)):
        lo = jnp.where(hot[gi] == 0, 1.0, 0.0).astype(BF16)
        hi = jnp.where(hot[gi] == vr, 1.0, 0.0).astype(BF16)
        rows = (dot(lo, tab[0]) + dot(hi, tab[1])).astype(BF16)
        for i in range(group):
            pk_send[g + i] = rows[i * slots:(i + 1) * slots]

    pk_recv[chip] = pk_send[chip]

    def send_rows(k, c):
        p = lax.rem(chip + k, n_chip)
        remote(pk_send.at[p], pk_recv.at[chip], pk_sem.at[0], pk_sem.at[1], 2 * p + core, h).start()
        return c

    lax.fori_loop(1, n_chip, send_rows, 0)

    for c in loads[2:]:
        c.wait()
    cos_t, sin_t = rope_t[0], rope_t[1]
    cos_s, sin_s = rope_s[0, pl.ds(s, 1), :], rope_s[1, pl.ds(s, 1), :]
    cosine = cos_t * cos_s - sin_t * sin_s
    sine = sin_t * cos_s + cos_t * sin_s
    lane128 = lax.broadcasted_iota(I32, (t_len, 128), 1)
    front = lax.rem(lane128, HD) < HD // 2
    sine = jnp.where(front, -sine, sine)

    def rope(x, scale):
        pieces = []
        for j in range(0, hw, 128):
            y = x[:, j:j + 128] * scale
            partner = jnp.where(front, pltpu.roll(y, 128 - HD // 2, 1), pltpu.roll(y, HD // 2, 1))
            pieces.append(y * cosine + partner * sine)
        return jnp.concatenate(pieces, axis=1)

    slots_iota = lax.broadcasted_iota(I32, (t_len, n_chip * slots), 1)
    unpack = jnp.where(jnp.broadcast_to(slot_key, slots_iota.shape) == slots_iota, 1.0, 0.0).astype(BF16)

    others = pk_recv.at[pl.ds(0, n_chip - 1)]
    pltpu.make_async_copy(others, others, pk_sem.at[1]).wait()
    packed = pk_recv[...].reshape(n_chip * slots, cw)
    st[0, 0] = dot(unpack, packed).astype(BF16)

    causal = lane[:, :t_len] <= sub[:, :t_len]
    causal2 = jnp.concatenate([causal, causal], axis=0)
    head_a = lane128 < HD
    ones = jnp.ones((t_len, 128), BF16)
    half_t = t_len // 2
    sends = []

    for layer in range(LAYERS):
        quarter = t_len // 4
        ups, dns, fws = [], [], []
        for c in range(4):
            a = pl.ds(c * quarter, quarter)
            e = 3 - c
            b = pl.ds(e * quarter, quarter)
            cu = remote(st.at[layer, 0, a], st.at[layer, 1, a], ag_s.at[layer, 0, c], ag_r.at[layer, 0, c], s, up)
            cd = remote(st.at[layer, 0, b], st.at[layer, 2, b], ag_s.at[layer, 1, e], ag_r.at[layer, 1, e], s, dn)
            cu.start()
            cd.start()
            ups.append(cu)
            dns.append(cd)

        def project(k, first):
            x = st[layer, k].astype(F32)
            rows = pl.ds(pl.multiple_of(blocks[k] * cw, cw), cw)
            cols = pl.ds(pl.multiple_of(blocks[k] * cw, 128), cw)
            gain = gain_v[pl.ds(layer, 1), cols]
            xg = (x * gain).astype(BF16)
            for i, w in enumerate((wk, wv, wq)):
                y = dot(xg, w[layer, rows, :])
                if first:
                    acc[i] = y
                else:
                    acc[i] += y
            return jnp.sum(x * x, axis=1, keepdims=True)

        for i in range(3):
            weights[layer, i].wait()
        square = project(0, True)
        for c in range(2):
            a = pl.ds(c * quarter, quarter)
            e = 3 - c
            b = pl.ds(e * quarter, quarter)
            ups[c].wait_recv()
            fu = remote(st.at[layer, 1, a], st.at[layer, 3, a], agf_s.at[layer, c], agf_r.at[layer, c], s, up)
            fu.start()
            dns[c].wait_recv()
            fd = remote(st.at[layer, 2, b], st.at[layer, 3, b], agf_s.at[layer, e], agf_r.at[layer, e], s, dn)
            fd.start()
            fws += [fu, fd]
        for c in range(2, 4):
            ups[c].wait_recv()
        square += project(1, False)
        for c in range(2, 4):
            dns[c].wait_recv()
        square += project(2, False)
        for f in fws:
            f.wait_recv()
        square += project(3, False)
        sends += ups + dns + fws
        scale = lax.rsqrt(square * (1.0 / (4 * cw)) + EPSILON)

        kv_own[layer, 0] = rope(acc[0], scale).astype(BF16)
        k_copy = remote(kv_own.at[layer, 0], kv_past.at[layer, 0], kv_s.at[layer, 0], kv_r.at[layer, 0], nxt, h)
        k_copy.start()
        kv_own[layer, 1] = (acc[1] * scale).astype(BF16)
        v_copy = remote(kv_own.at[layer, 1], kv_past.at[layer, 1], kv_s.at[layer, 1], kv_r.at[layer, 1], nxt, h)
        v_copy.start()
        sends += [k_copy, v_copy]
        q_own[...] = (rope(acc[2], scale) * HD ** (-0.5)).astype(BF16)

        def queries_of(j):
            q = q_own[:, j:j + 128]
            none = jnp.zeros_like(q)
            return jnp.concatenate([jnp.where(head_a, q, none), jnp.where(head_a, none, q)], axis=0)

        for i, j in enumerate(range(0, hw, 128)):
            scores = dot_nt(queries_of(j), kv_own[layer, 0, :, j:j + 128])
            scores = jnp.where(causal2, scores, -1e30)
            top = jnp.max(scores, axis=1, keepdims=True)
            e = jnp.exp(scores - top).astype(BF16)
            values = jnp.concatenate([kv_own[layer, 1, :, j:j + 128], ones], axis=1)
            o_part[i] = dot(e, values)
            mx_part[i] = jnp.broadcast_to(top, (2 * t_len, 128))
        k_copy.wait_recv()
        v_copy.wait_recv()
        for i, j in enumerate(range(0, hw, 128)):
            scores = dot_nt(queries_of(j), kv_past[layer, 0, :, j:j + 128])
            scores = jnp.where(s > 0, scores, -1e30)
            old = mx_part[i]
            top = jnp.maximum(old, jnp.max(scores, axis=1, keepdims=True))
            e = jnp.exp(scores - top).astype(BF16)
            keep = jnp.exp(old - top)
            values = jnp.concatenate([kv_past[layer, 1, :, j:j + 128], ones], axis=1)
            o = dot(e, values)
            num = o_part[i, :, :128] * keep + o[:, :128]
            den = o_part[i, :, 128:] * keep + o[:, 128:]
            m = num / den
            mixed[:, j:j + 128] = jnp.where(head_a, m[:t_len], m[t_len:]).astype(BF16)

        weights[layer, 3].wait()
        last = layer == LAYERS - 1
        part, comb, frecv, rrecv = (
            (part1, comb1, frecv1, rrecv1) if last else (part0, comb0, frecv0, rrecv0)
        )
        n_row = part.shape[1]
        lo, hi = pl.ds(0, n_row // 2), pl.ds(n_row // 2, n_row // 2)

        def send(i, src, dst, to):
            c = remote(src, dst, rs_s.at[layer, i], rs_r.at[layer, i], s, to)
            c.start()
            sends.append(c)
            return c

        def far():
            return [
                send(0, part.at[opp, lo], frecv.at[0], up),
                send(1, part.at[opp, hi], frecv.at[1], dn),
            ]

        if last:
            for b in range(4):
                y = dot(mixed[...], wo[layer, :, b * cw:(b + 1) * cw]).astype(BF16)
                for d in range(4):
                    part[d, :, b * cw:(b + 1) * cw] = y[d * n_row:(d + 1) * n_row]
            f = far()
        else:
            for b in (opp, up, dn, h):
                y = dot(mixed[...], wo[layer, :, pl.ds(pl.multiple_of(b * cw, 128), cw)])
                part[b] = y.astype(BF16)
                if b is opp:
                    f = far()
        r = [
            send(2, part.at[up, hi], rrecv.at[0, hi], up),
            send(3, part.at[dn, lo], rrecv.at[1, lo], dn),
        ]
        f[0].wait_recv()
        comb[0] = (part[up, lo].astype(F32) + frecv[0].astype(F32)).astype(BF16)
        r.append(send(4, comb.at[0], rrecv.at[0, lo], up))
        f[1].wait_recv()
        comb[1] = (part[dn, hi].astype(F32) + frecv[1].astype(F32)).astype(BF16)
        r.append(send(5, comb.at[1], rrecv.at[1, hi], dn))
        for c in r:
            c.wait_recv()
        total = part[h].astype(F32) + rrecv[0].astype(F32) + rrecv[1].astype(F32)
        if last:
            for k in range(4):
                cols = pl.ds(pl.multiple_of(blocks[k] * cw, 128), cw)
                rows = pl.ds(pl.multiple_of(h * n_row, n_row), n_row)
                out_ref[:, cols] = st[layer, k, rows, :].astype(F32)
            out_ref[...] += total
        else:
            st[layer + 1, 0] = (st[layer, 0].astype(F32) + total).astype(BF16)

    flag_copy.wait()
    flag_ref[0, 0] = jnp.max(jnp.maximum(flag_send[...], flag_recv[...]))
    tab_copy.wait_send()
    others = req_send.at[pl.ds(0, n_chip - 1)]
    pltpu.make_async_copy(others, others, req_sem.at[0]).wait()
    others = pk_send.at[pl.ds(0, n_chip - 1)]
    pltpu.make_async_copy(others, others, pk_sem.at[0]).wait()
    for c in sends:
        c.wait_send()


def rotary_tables(n_seg, t_len):
    freq = 10000.0 ** (-np.arange(HD // 2, dtype=np.float64) / (HD // 2))
    freq = np.tile(freq, 128 // (HD // 2))[None]
    local = np.arange(t_len, dtype=np.float64)[:, None] * freq
    start = (np.arange(n_seg, dtype=np.float64) * t_len)[:, None] * freq
    both = lambda a: np.stack([np.cos(a), np.sin(a)]).astype(np.float32)
    return both(local), both(start)


def run(slots, n_seg, token_ids, embed_table, norm_gains, query_weight, key_weight, value_weight, out_weight):
    t_len = token_ids.shape[0]
    vr, cw = embed_table.shape
    hw = query_weight.shape[2]
    n_chip = n_seg // 2
    rope_t, rope_s = rotary_tables(n_seg, t_len)
    rows = t_len // 4
    vmem = pltpu.VMEM
    dma = pltpu.SemaphoreType.DMA
    any_spec = pl.BlockSpec(memory_space=pl.ANY)
    vmem_spec = pl.BlockSpec(memory_space=pltpu.VMEM)
    return pl.pallas_call(
        functools.partial(kernel, slots, n_seg, vr, t_len, cw, hw),
        out_shape=(
            jax.ShapeDtypeStruct((rows, 4 * cw), F32),
            jax.ShapeDtypeStruct((1, 1), I32),
        ),
        in_specs=[any_spec] * 9,
        out_specs=(vmem_spec, pl.BlockSpec(memory_space=pltpu.SMEM)),
        scratch_shapes=[
            vmem((1, t_len), I32),
            vmem(norm_gains.shape, F32),
            vmem(rope_t.shape, F32),
            vmem(rope_s.shape, F32),
            vmem((2, vr, cw), BF16),
            vmem(query_weight.shape, BF16),
            vmem(key_weight.shape, BF16),
            vmem(value_weight.shape, BF16),
            vmem(out_weight.shape, BF16),
            vmem((n_chip, 1, t_len), I32),
            vmem((n_chip, 1, t_len), I32),
            vmem((8, t_len), I32),
            vmem((8, t_len), I32),
            vmem((n_chip, slots, cw), BF16),
            vmem((n_chip, slots, cw), BF16),
            vmem((LAYERS, 4, t_len, cw), BF16),
            vmem((3, t_len, hw), F32),
            vmem((LAYERS, 2, t_len, hw), BF16),
            vmem((LAYERS, 2, t_len, hw), BF16),
            vmem((t_len, hw), BF16),
            vmem((hw // 128, 2 * t_len, 256), F32),
            vmem((hw // 128, 2 * t_len, 128), F32),
            vmem((t_len, hw), BF16),
            vmem((4, t_len, cw), BF16),
            vmem((4, rows, 4 * cw), BF16),
            vmem((2, t_len // 2, cw), BF16),
            vmem((2, rows // 2, 4 * cw), BF16),
            vmem((2, t_len // 2, cw), BF16),
            vmem((2, rows // 2, 4 * cw), BF16),
            vmem((2, t_len, cw), BF16),
            vmem((2, rows, 4 * cw), BF16),
            dma((5,)),
            dma((LAYERS, 4)),
            dma((2,)),
            dma((2,)),
            dma((2,)),
            dma((2,)),
            dma((LAYERS, 2, 4)),
            dma((LAYERS, 2, 4)),
            dma((LAYERS, 4)),
            dma((LAYERS, 4)),
            dma((LAYERS, 2)),
            dma((LAYERS, 2)),
            dma((LAYERS, 6)),
            dma((LAYERS, 6)),
        ],
        compiler_params=pltpu.CompilerParams(
            collective_id=int(slots == ALL_SLOTS), has_side_effects=True, vmem_limit_bytes=56 * 2 ** 20
        ),
        name="decoder",
    )(
        token_ids.reshape(1, t_len), embed_table, norm_gains,
        query_weight, key_weight, value_weight, out_weight,
        jnp.asarray(rope_t), jnp.asarray(rope_s),
    )


def body(n_seg, *arrays):
    out, flag = run(SLOTS, n_seg, *arrays)
    return lax.cond(
        flag[0, 0] > 0,
        lambda: run(ALL_SLOTS, n_seg, *arrays)[0].astype(BF16),
        lambda: out.astype(BF16),
    )


def solution(mesh):
    placed = (
        P("seg"),
        P("seg", "head"),
        P(),
        P(None, None, "head"),
        P(None, None, "head"),
        P(None, None, "head"),
        P(None, "head", None),
    )
    return jax.shard_map(
        functools.partial(body, mesh.shape["seg"]),
        mesh=mesh, in_specs=placed, out_specs=P(("seg", "head"), None), check_vma=False,
    )
```

```python
import functools

import jax
import jax.numpy as jnp
import numpy as np
from jax import lax
from jax.experimental import pallas as pl
from jax.experimental.pallas import tpu as pltpu
from jax.sharding import PartitionSpec as P

HD = 64
LAYERS = 2
EPSILON = 1e-05
SLOTS, ALL_SLOTS = 24, 128
MESH = pl.DeviceIdType.MESH
F32 = jnp.float32
BF16 = jnp.bfloat16
I32 = jnp.int32


def dot(a, b):
    return jnp.dot(a, b, preferred_element_type=F32)


def dot_nt(a, b):
    return lax.dot_general(a, b, (((1,), (1,)), ((), ())), preferred_element_type=F32)


def plane(n_chip):
    nx, nz = (4, n_chip // 4) if n_chip % 4 == 0 else (1, n_chip)
    far = lambda d, n: min(d, n - d)
    slots = [
        (dx * nz + dz, dx, dz, (-dx) % nx * nz + (-dz) % nz) for dx in range(nx) for dz in range(nz)
    ]
    return nx, nz, sorted(slots, key=lambda o: far(o[1], nx) + far(o[2], nz))


def kernel(
    slots, n_seg, vr, t_len, cw, hw, f_cuts,
    ids_hbm, tab_hbm, gain_hbm, wq_hbm, wk_hbm, wv_hbm, wo_hbm, rope_t_hbm, rope_s_hbm,
    out_ref, flag_ref,
    ids_v, gain_v, rope_t, rope_s, tab, wq, wk, wv, wo,
    req_send, req_recv, flag_send, flag_recv, hot, pk_send, pk_recv,
    st, acc, kv_own, kv_past, q_own, o_part, mx_part, mixed,
    part0, part1, frecv0, frecv1, comb0, comb1, rrecv0, rrecv1,
    l_sem, w_sem, tab_sem, req_s, req_r, flag_sem, pk_s, pk_r,
    ag_s, ag_r, agf_s, agf_r, kv_s, kv_r, rs_s, rs_r,
):
    s = lax.axis_index("seg")
    h = lax.axis_index("head")
    chip, core = s // 2, lax.rem(s, 2)
    n_chip = n_seg // 2
    nx, nz, offsets = plane(n_chip)
    x, z = chip // nz, lax.rem(chip, nz)
    up, dn, opp = lax.rem(h + 1, 4), lax.rem(h + 3, 4), lax.rem(h + 2, 4)
    sib = s + 1 - 2 * core
    nxt, prv = lax.rem(s + 1, n_seg), lax.rem(s + n_seg - 1, n_seg)
    blocks = (h, dn, up, opp)

    def chip_at(dx, dz):
        return lax.rem(x + dx, nx) * nz + lax.rem(z + dz, nz)

    def remote(src, dst, ss, rs, seg, head):
        return pltpu.make_async_remote_copy(
            src_ref=src, dst_ref=dst, send_sem=ss, recv_sem=rs,
            device_id=(seg, head), device_id_type=MESH,
        )

    bar = pltpu.get_barrier_semaphore()

    def hello(seg, head):
        pl.semaphore_signal(bar, inc=1, device_id=(seg, head), device_id_type=MESH)

    for _, dx, dz, _ in offsets[:0:-1]:
        hello(2 * chip_at(dx, dz) + core, h)
    for other in (up, dn):
        hello(s, other)
    hello(sib, h)
    hello(prv, h)

    loads = [
        pltpu.make_async_copy(a, b, l_sem.at[i])
        for i, (a, b) in enumerate(
            [(ids_hbm, ids_v), (tab_hbm, tab.at[core]), (gain_hbm, gain_v),
             (rope_t_hbm, rope_t), (rope_s_hbm, rope_s)]
        )
    ]
    for c in loads:
        c.start()
    weights = {}
    for layer in range(LAYERS):
        for i, (a, b) in enumerate([(wk_hbm, wk), (wv_hbm, wv), (wq_hbm, wq), (wo_hbm, wo)]):
            c = pltpu.make_async_copy(a.at[layer], b.at[layer], w_sem.at[layer, i])
            c.start()
            weights[layer, i] = c

    loads[0].wait()
    sub = lax.broadcasted_iota(I32, (t_len, t_len), 0)
    lane = lax.broadcasted_iota(I32, (t_len, t_len), 1)
    idr = jnp.broadcast_to(ids_v[...], (t_len, t_len))
    idc = idr.T

    def chip_of(ids):
        return ((ids.astype(F32) + 0.5) * (1.0 / (2 * vr))).astype(I32)

    pr, pc = chip_of(idr), chip_of(idc)
    same = idr == idc
    one = jnp.ones((), I32)
    zero = jnp.zeros((), I32)
    dup_row = jnp.sum(jnp.where(same & (sub < lane), one, zero), axis=0, keepdims=True)
    dup_col = jnp.sum(jnp.where(same & (lane < sub), one, zero), axis=1, keepdims=True)
    first_row, first_col = dup_row == 0, dup_col == 0
    peer = pr == pc
    rank_row = jnp.sum(jnp.where(peer & (idc < idr) & first_col, one, zero), axis=0, keepdims=True)
    rank_col = jnp.sum(jnp.where(peer & (idr < idc) & first_row, one, zero), axis=1, keepdims=True)
    full = jnp.where(jnp.max(rank_row, axis=1, keepdims=True) >= slots, one, zero)
    wanted = jnp.where(first_col, pc[:, 0:1] * t_len + rank_col, -1)
    wanted = jnp.broadcast_to(wanted, (t_len, t_len)) - lane
    local_id = idc - 2 * vr * pc + 1
    lane_row = lane[0:1]
    for slot, dx, dz, _ in offsets:
        row = jnp.where(wanted == chip_at(dx, dz) * t_len, local_id, zero)
        row = jnp.sum(row, axis=0, keepdims=True) - 1
        req_send[slot] = jnp.where(lane_row == t_len - 1, full, row) if slots < t_len else row
    req_recv[0] = req_send[0]

    px = sum(jnp.where(pc >= i * nz, one, zero) for i in range(1, nx)) if nx > 1 else jnp.zeros_like(pc)
    rx, rz = px - x, pc - px * nz - z
    rel = jnp.where(rx < 0, rx + nx, rx) * nz + jnp.where(rz < 0, rz + nz, rz)
    slot_key = rel[:, 0:1] * slots + rank_col
    slots_iota = lax.broadcasted_iota(I32, (t_len, n_chip * slots), 1)
    unpack = jnp.where(jnp.broadcast_to(slot_key, slots_iota.shape) == slots_iota, 1.0, 0.0).astype(BF16)

    @pl.when(s == 0)
    def _():
        kv_past[...] = jnp.zeros_like(kv_past)

    pl.semaphore_wait(bar, 2 + 2 + n_chip - 1)

    group = min(4, n_chip)
    group_of = {o[0]: i // group for i, o in enumerate(offsets)}
    for slot, dx, dz, back in offsets[:0:-1]:
        remote(
            req_send.at[slot], req_recv.at[back], req_s.at[0], req_r.at[group_of[back]],
            2 * chip_at(dx, dz) + core, h,
        ).start()
    tab_copy = remote(tab_hbm, tab.at[core], tab_sem.at[0], tab_sem.at[1], sib, h)
    tab_copy.start()
    loads[1].wait()
    row_iota = lax.broadcasted_iota(I32, (slots, vr), 1)

    pk_copies = {}
    for f, (f0, f1) in enumerate(f_cuts):
        cols = pl.ds(f0, f1 - f0)
        for g in range(n_chip // group):
            members = offsets[g * group:(g + 1) * group]
            rows = pl.ds(g * group * slots, group * slots)
            if f == 0:
                came = req_recv.at[pl.ds(0, sum(o[0] != 0 for o in members))]
                pltpu.make_async_copy(came, came, req_r.at[g]).wait()
                asked = jnp.concatenate(
                    [req_recv[o[0]] for o in members] + [jnp.zeros((t_len - group, t_len), I32)], axis=0
                ).T
                away = jnp.concatenate(
                    [jnp.broadcast_to(asked[:slots, i:i + 1], (slots, vr)) - row_iota for i in range(group)], axis=0
                )
                if g == 0:
                    tab_copy.wait_recv()
                hot[0, rows] = jnp.where(away == 0, 1.0, 0.0).astype(BF16)
                hot[1, rows] = jnp.where(away == vr, 1.0, 0.0).astype(BF16)
            found = dot(hot[0, rows], tab[0, :, cols]) + dot(hot[1, rows], tab[1, :, cols])
            for i, (slot, dx, dz, back) in enumerate(members):
                piece = found[i * slots:(i + 1) * slots].astype(BF16)
                if slot == 0:
                    pk_recv[0, :, cols] = piece
                else:
                    pk_send[slot, :, cols] = piece
                    remote(
                        pk_send.at[slot, :, cols], pk_recv.at[back, :, cols], pk_s.at[f], pk_r.at[f],
                        2 * chip_at(dx, dz) + core, h,
                    ).start()

    reqs = jnp.concatenate([req_recv[p] for p in range(n_chip)], axis=0)
    any_full = jnp.max(reqs, axis=0, keepdims=True)
    any_full = jnp.max(jnp.where(lane_row == t_len - 1, any_full, zero), axis=1, keepdims=True)
    flag_send[...] = jnp.broadcast_to(any_full, (8, t_len))
    flag_copy = remote(flag_send, flag_recv, flag_sem.at[0], flag_sem.at[1], sib, h)
    flag_copy.start()

    for c in loads[2:]:
        c.wait()
    cos_t, sin_t = rope_t[0], rope_t[1]
    cos_s, sin_s = rope_s[0, pl.ds(s, 1), :], rope_s[1, pl.ds(s, 1), :]
    cosine = cos_t * cos_s - sin_t * sin_s
    sine = sin_t * cos_s + cos_t * sin_s
    lane128 = lax.broadcasted_iota(I32, (t_len, 128), 1)
    front = lax.rem(lane128, HD) < HD // 2
    sine = jnp.where(front, -sine, sine)

    def rope(x, scale):
        pieces = []
        for j in range(0, hw, 128):
            y = x[:, j:j + 128] * scale
            partner = jnp.where(front, pltpu.roll(y, 128 - HD // 2, 1), pltpu.roll(y, HD // 2, 1))
            pieces.append(y * cosine + partner * sine)
        return jnp.concatenate(pieces, axis=1)

    causal = lane[:, :t_len] <= sub[:, :t_len]
    causal2 = jnp.concatenate([causal, causal], axis=0)
    head_a = lane128 < HD
    ones = jnp.ones((t_len, 128), BF16)
    sends = []

    def halves(region):
        r0, r1, c0, c1 = region
        mid, cols = (r0 + r1) // 2, pl.ds(c0, c1 - c0)
        return (pl.ds(r0, mid - r0), cols), (pl.ds(mid, r1 - mid), cols)

    def share(layer, i, region):
        a, b = halves(region)
        own, low, high = st.at[layer, 0], st.at[layer, 1], st.at[layer, 2]

        def both(k, part):
            cu = remote(own.at[part], low.at[part], ag_s.at[layer, i, 0, k], ag_r.at[layer, i, 0, k], s, up)
            cd = remote(own.at[part], high.at[part], ag_s.at[layer, i, 1, k], ag_r.at[layer, i, 1, k], s, dn)
            return cu, cd

        (ua, da), (ub, db) = both(0, a), both(1, b)
        for c in (ua, db, ub, da):
            c.start()
        sends.extend([ua, db, ub, da])
        return ua, da, ub, db

    def pass_on(layer, i, region, copies):
        ua, da, ub, db = copies
        a, b = halves(region)
        low, high, far = st.at[layer, 1], st.at[layer, 2], st.at[layer, 3]
        fu = remote(low.at[a], far.at[a], agf_s.at[layer, i, 0], agf_r.at[layer, i, 0], s, up)
        fd = remote(high.at[b], far.at[b], agf_s.at[layer, i, 1], agf_r.at[layer, i, 1], s, dn)
        ua.wait_recv()
        fu.start()
        db.wait_recv()
        fd.start()
        sends.extend([fu, fd])
        return fu, fd

    def project(layer, k, c0, c1, first):
        start = blocks[k] * cw + c0
        x = st[layer, k, :, c0:c1].astype(F32)
        rows = pl.ds(pl.multiple_of(start, 128), c1 - c0)
        gain = gain_v[pl.ds(layer, 1), rows]
        xg = (x * gain).astype(BF16)
        for i, w in enumerate((wk, wv, wq)):
            y = dot(xg, w[layer, rows, :])
            if first:
                acc[i] = y
            else:
                acc[i] += y
        return jnp.sum(x * x, axis=1, keepdims=True)

    for layer in range(LAYERS):
        last = layer == LAYERS - 1
        if layer == 0:
            regions = [(0, t_len, f0, f1) for f0, f1 in f_cuts]
            copies, passed = [], []
            square = jnp.zeros((t_len, 1), F32)
            for i, region in enumerate(regions):
                cols = pl.ds(region[2], region[3] - region[2])
                came = pk_recv.at[pl.ds(1, n_chip - 1), :, cols]
                pltpu.make_async_copy(came, came, pk_r.at[i]).wait()
                packed = pk_recv[:, :, cols].reshape(n_chip * slots, region[3] - region[2])
                st[0, 0, :, cols] = dot(unpack, packed).astype(BF16)
                copies.append(share(layer, i, region))
                if i == 0:
                    for w in range(3):
                        weights[layer, w].wait()
                square += project(layer, 0, *region[2:], i == 0)
            passed = [pass_on(layer, i, region, copies[i]) for i, region in enumerate(regions)]
            for i, region in enumerate(regions):
                ua, da, ub, db = copies[i]
                ub.wait_recv()
                square += project(layer, 1, *region[2:], False)
                da.wait_recv()
                square += project(layer, 2, *region[2:], False)
                for c in passed[i]:
                    c.wait_recv()
                square += project(layer, 3, *region[2:], False)
        else:
            for w in range(3):
                weights[layer, w].wait()
            square = project(layer, 0, 0, cw, True)
            passed = [pass_on(layer, i, region, copies[i]) for i, region in enumerate(regions)]
            for ua, da, ub, db in copies:
                ub.wait_recv()
            square += project(layer, 1, 0, cw, False)
            for ua, da, ub, db in copies:
                da.wait_recv()
            square += project(layer, 2, 0, cw, False)
            for pair in passed:
                for c in pair:
                    c.wait_recv()
            square += project(layer, 3, 0, cw, False)
        scale = lax.rsqrt(square * (1.0 / (4 * cw)) + EPSILON)

        kv_copies = [
            remote(kv_own.at[layer, i], kv_past.at[layer, i], kv_s.at[layer, i], kv_r.at[layer, i], nxt, h)
            for i in range(2)
        ]

        def send_on(i):
            @pl.when(s < n_seg - 1)
            def _():
                kv_copies[i].start()

        kv_own[layer, 0] = rope(acc[0], scale).astype(BF16)
        send_on(0)
        kv_own[layer, 1] = (acc[1] * scale).astype(BF16)
        send_on(1)
        q_own[...] = (rope(acc[2], scale) * HD ** (-0.5)).astype(BF16)

        def queries_of(j):
            q = q_own[:, j:j + 128]
            none = jnp.zeros_like(q)
            return jnp.concatenate([jnp.where(head_a, q, none), jnp.where(head_a, none, q)], axis=0)

        for i, j in enumerate(range(0, hw, 128)):
            scores = dot_nt(queries_of(j), kv_own[layer, 0, :, j:j + 128])
            scores = jnp.where(causal2, scores, -1e30)
            top = jnp.max(scores, axis=1, keepdims=True)
            e = jnp.exp(scores - top).astype(BF16)
            values = jnp.concatenate([kv_own[layer, 1, :, j:j + 128], ones], axis=1)
            o_part[i] = dot(e, values)
            mx_part[i] = jnp.broadcast_to(top, (2 * t_len, 128))

        @pl.when(s > 0)
        def _():
            kv_copies[0].wait_recv()
            kv_copies[1].wait_recv()

        for i, j in enumerate(range(0, hw, 128)):
            scores = dot_nt(queries_of(j), kv_past[layer, 0, :, j:j + 128])
            scores = jnp.where(s > 0, scores, -1e30)
            old = mx_part[i]
            top = jnp.maximum(old, jnp.max(scores, axis=1, keepdims=True))
            e = jnp.exp(scores - top).astype(BF16)
            keep = jnp.exp(old - top)
            values = jnp.concatenate([kv_past[layer, 1, :, j:j + 128], ones], axis=1)
            o = dot(e, values)
            num = o_part[i, :, :128] * keep + o[:, :128]
            den = o_part[i, :, 128:] * keep + o[:, 128:]
            m = num / den
            mixed[:, j:j + 128] = jnp.where(head_a, m[:t_len], m[t_len:]).astype(BF16)

        weights[layer, 3].wait()
        part, comb, frecv, rrecv = (
            (part1, comb1, frecv1, rrecv1) if last else (part0, comb0, frecv0, rrecv0)
        )
        n_row, n_col = part.shape[1:]
        if last:
            regions = [(0, n_row, 0, n_col // 2), (0, n_row, n_col // 2, n_col)]
        else:
            regions = [(0, n_row // 2, 0, n_col), (n_row // 2, n_row, 0, n_col)]

        def send(i, k, src, dst, to):
            c = remote(src, dst, rs_s.at[layer, i, k], rs_r.at[layer, i, k], s, to)
            c.start()
            sends.append(c)
            return c

        def far(i):
            a, b = halves(regions[i])
            return (
                send(i, 0, part.at[opp].at[a], frecv.at[0].at[a], up),
                send(i, 1, part.at[opp].at[b], frecv.at[1].at[b], dn),
            )

        def near(i):
            a, b = halves(regions[i])
            return (
                send(i, 2, part.at[up].at[b], rrecv.at[0].at[b], up),
                send(i, 3, part.at[dn].at[a], rrecv.at[1].at[a], dn),
            )

        def join(i, f):
            a, b = halves(regions[i])
            f[0].wait_recv()
            comb[(0,) + a] = (part[(up,) + a].astype(F32) + frecv[(0,) + a].astype(F32)).astype(BF16)
            cu = send(i, 4, comb.at[0].at[a], rrecv.at[0].at[a], up)
            f[1].wait_recv()
            comb[(1,) + b] = (part[(dn,) + b].astype(F32) + frecv[(1,) + b].astype(F32)).astype(BF16)
            return cu, send(i, 5, comb.at[1].at[b], rrecv.at[1].at[b], dn)

        if last:
            fars, nears = [], []
            for b in range(4):
                y = dot(mixed[...], wo[layer, :, b * cw:(b + 1) * cw]).astype(BF16)
                for d in range(4):
                    part[d, :, b * cw:(b + 1) * cw] = y[d * n_row:(d + 1) * n_row]
                if b % 2 == 1:
                    fars.append(far(b // 2))
                    nears.append(near(b // 2))
        else:
            for b in (opp, up, dn, h):
                y = dot(mixed[...], wo[layer, :, pl.ds(pl.multiple_of(b * cw, 128), cw)])
                part[b] = y.astype(BF16)
                if b is opp:
                    fars = [far(0), far(1)]
                if b is dn:
                    nears = [near(0), near(1)]
        joined = [join(i, fars[i]) for i in range(2)]
        copies = []
        for i, region in enumerate(regions):
            for c in nears[i] + joined[i]:
                c.wait_recv()
            r0, r1, c0, c1 = region
            at = (slice(r0, r1), slice(c0, c1))
            total = part[(h,) + at].astype(F32) + rrecv[(0,) + at].astype(F32) + rrecv[(1,) + at].astype(F32)
            if last:
                rows = pl.ds(pl.multiple_of(h * n_row, n_row), n_row)
                if i == 0:
                    for k in range(4):
                        cols = pl.ds(pl.multiple_of(blocks[k] * cw, 128), cw)
                        out_ref[:, cols] = st[layer, k, rows, :].astype(F32)
                out_ref[at] += total
            else:
                st[(layer + 1, 0) + at] = (st[(layer, 0) + at].astype(F32) + total).astype(BF16)
                copies.append(share(layer + 1, i, region))

        @pl.when(s < n_seg - 1)
        def _():
            for c in kv_copies:
                c.wait_send()

    flag_copy.wait()
    flag_ref[0, 0] = jnp.max(jnp.maximum(flag_send[...], flag_recv[...]))
    tab_copy.wait_send()
    others = req_send.at[pl.ds(0, n_chip - 1)]
    pltpu.make_async_copy(others, others, req_s.at[0]).wait()
    for f, (f0, f1) in enumerate(f_cuts):
        others = pk_send.at[pl.ds(1, n_chip - 1), :, pl.ds(f0, f1 - f0)]
        pltpu.make_async_copy(others, others, pk_s.at[f]).wait()
    for c in sends:
        c.wait_send()


def rotary_tables(n_seg, t_len):
    freq = 10000.0 ** (-np.arange(HD // 2, dtype=np.float64) / (HD // 2))
    freq = np.tile(freq, 128 // (HD // 2))[None]
    local = np.arange(t_len, dtype=np.float64)[:, None] * freq
    start = (np.arange(n_seg, dtype=np.float64) * t_len)[:, None] * freq
    both = lambda a: np.stack([np.cos(a), np.sin(a)]).astype(np.float32)
    return both(local), both(start)


def run(slots, n_seg, token_ids, embed_table, norm_gains, query_weight, key_weight, value_weight, out_weight):
    t_len = token_ids.shape[0]
    vr, cw = embed_table.shape
    hw = query_weight.shape[2]
    n_chip = n_seg // 2
    rope_t, rope_s = rotary_tables(n_seg, t_len)
    f_cuts = [(0, 384), (384, cw)] if cw > 384 else [(0, cw)]
    n_cut = max(2, len(f_cuts))
    rows = t_len // 4
    vmem = pltpu.VMEM
    dma = pltpu.SemaphoreType.DMA
    any_spec = pl.BlockSpec(memory_space=pl.ANY)
    vmem_spec = pl.BlockSpec(memory_space=pltpu.VMEM)
    return pl.pallas_call(
        functools.partial(kernel, slots, n_seg, vr, t_len, cw, hw, f_cuts),
        out_shape=(
            jax.ShapeDtypeStruct((rows, 4 * cw), F32),
            jax.ShapeDtypeStruct((1, 1), I32),
        ),
        in_specs=[any_spec] * 9,
        out_specs=(vmem_spec, pl.BlockSpec(memory_space=pltpu.SMEM)),
        scratch_shapes=[
            vmem((1, t_len), I32),
            vmem(norm_gains.shape, F32),
            vmem(rope_t.shape, F32),
            vmem(rope_s.shape, F32),
            vmem((2, vr, cw), BF16),
            vmem(query_weight.shape, BF16),
            vmem(key_weight.shape, BF16),
            vmem(value_weight.shape, BF16),
            vmem(out_weight.shape, BF16),
            vmem((n_chip, 1, t_len), I32),
            vmem((n_chip, 1, t_len), I32),
            vmem((8, t_len), I32),
            vmem((8, t_len), I32),
            vmem((2, n_chip * slots, vr), BF16),
            vmem((n_chip, slots, cw), BF16),
            vmem((n_chip, slots, cw), BF16),
            vmem((LAYERS, 4, t_len, cw), BF16),
            vmem((3, t_len, hw), F32),
            vmem((LAYERS, 2, t_len, hw), BF16),
            vmem((LAYERS, 2, t_len, hw), BF16),
            vmem((t_len, hw), BF16),
            vmem((hw // 128, 2 * t_len, 256), F32),
            vmem((hw // 128, 2 * t_len, 128), F32),
            vmem((t_len, hw), BF16),
            vmem((4, t_len, cw), BF16),
            vmem((4, rows, 4 * cw), BF16),
            vmem((2, t_len, cw), BF16),
            vmem((2, rows, 4 * cw), BF16),
            vmem((2, t_len, cw), BF16),
            vmem((2, rows, 4 * cw), BF16),
            vmem((2, t_len, cw), BF16),
            vmem((2, rows, 4 * cw), BF16),
            dma((5,)),
            dma((LAYERS, 4)),
            dma((2,)),
            dma((1,)),
            dma((n_chip,)),
            dma((2,)),
            dma((n_cut,)),
            dma((n_cut,)),
            dma((LAYERS, n_cut, 2, 2)),
            dma((LAYERS, n_cut, 2, 2)),
            dma((LAYERS, n_cut, 2)),
            dma((LAYERS, n_cut, 2)),
            dma((LAYERS, 2)),
            dma((LAYERS, 2)),
            dma((LAYERS, 2, 6)),
            dma((LAYERS, 2, 6)),
        ],
        compiler_params=pltpu.CompilerParams(
            collective_id=int(slots == ALL_SLOTS), has_side_effects=True, vmem_limit_bytes=56 * 2 ** 20
        ),
        name="decoder",
    )(
        token_ids.reshape(1, t_len), embed_table, norm_gains,
        query_weight, key_weight, value_weight, out_weight,
        jnp.asarray(rope_t), jnp.asarray(rope_s),
    )


def body(n_seg, *arrays):
    out, flag = run(SLOTS, n_seg, *arrays)
    return lax.cond(
        flag[0, 0] > 0,
        lambda: run(ALL_SLOTS, n_seg, *arrays)[0].astype(BF16),
        lambda: out.astype(BF16),
    )


def solution(mesh):
    placed = (
        P("seg"),
        P("seg", "head"),
        P(),
        P(None, None, "head"),
        P(None, None, "head"),
        P(None, None, "head"),
        P(None, "head", None),
    )
    return jax.shard_map(
        functools.partial(body, mesh.shape["seg"]),
        mesh=mesh, in_specs=placed, out_specs=P(("seg", "head"), None), check_vma=False,
    )
```

```python
import functools

import jax
import jax.numpy as jnp
import numpy as np
from jax import lax
from jax.experimental import pallas as pl
from jax.experimental.pallas import tpu as pltpu
from jax.sharding import PartitionSpec as P

HD = 64
LAYERS = 2
EPSILON = 1e-05
SLOTS, ALL_SLOTS = 24, 128
MESH = pl.DeviceIdType.MESH
F32 = jnp.float32
BF16 = jnp.bfloat16
I32 = jnp.int32


def dot(a, b):
    return jnp.dot(a, b, preferred_element_type=F32)


def dot_nt(a, b):
    return lax.dot_general(a, b, (((1,), (1,)), ((), ())), preferred_element_type=F32)


def plane(n_chip):
    nx, nz = (4, n_chip // 4) if n_chip % 4 == 0 else (1, n_chip)
    far = lambda d, n: min(d, n - d)
    slots = [
        (dx * nz + dz, dx, dz, (-dx) % nx * nz + (-dz) % nz) for dx in range(nx) for dz in range(nz)
    ]
    return nx, nz, sorted(slots, key=lambda o: far(o[1], nx) + far(o[2], nz))


def kernel(
    slots, n_seg, vr, t_len, cw, hw, f_cuts,
    ids_hbm, tab_hbm, gain_hbm, wq_hbm, wk_hbm, wv_hbm, wo_hbm, rope_t_hbm, rope_s_hbm,
    out_ref, flag_ref,
    ids_v, gain_v, rope_t, rope_s, tab, wq, wk, wv, wo,
    req_send, req_recv, flag_send, flag_recv, hot, pk_send, pk_recv,
    st, acc, kv_own, kv_past, q_own, o_part, mx_part, mixed,
    part0, part1, frecv0, frecv1, comb0, comb1, rrecv0, rrecv1,
    l_sem, w_sem, tab_sem, req_s, req_r, flag_sem, pk_s, pk_r,
    ag_s, ag_r, agf_s, agf_r, kv_s, kv_r, rs_s, rs_r,
):
    s = lax.axis_index("seg")
    h = lax.axis_index("head")
    chip, core = s // 2, lax.rem(s, 2)
    n_chip = n_seg // 2
    nx, nz, offsets = plane(n_chip)
    x, z = chip // nz, lax.rem(chip, nz)
    up, dn, opp = lax.rem(h + 1, 4), lax.rem(h + 3, 4), lax.rem(h + 2, 4)
    sib = s + 1 - 2 * core
    nxt, prv = lax.rem(s + 1, n_seg), lax.rem(s + n_seg - 1, n_seg)
    blocks = (h, dn, up, opp)

    def chip_at(dx, dz):
        return lax.rem(x + dx, nx) * nz + lax.rem(z + dz, nz)

    def remote(src, dst, ss, rs, seg, head):
        return pltpu.make_async_remote_copy(
            src_ref=src, dst_ref=dst, send_sem=ss, recv_sem=rs,
            device_id=(seg, head), device_id_type=MESH,
        )

    bar = pltpu.get_barrier_semaphore()

    def hello(seg, head):
        pl.semaphore_signal(bar, inc=1, device_id=(seg, head), device_id_type=MESH)

    for _, dx, dz, _ in offsets[:0:-1]:
        hello(2 * chip_at(dx, dz) + core, h)
    for other in (up, dn):
        hello(s, other)
    hello(s, opp)
    hello(sib, h)
    hello(prv, h)

    loads = [
        pltpu.make_async_copy(a, b, l_sem.at[i])
        for i, (a, b) in enumerate(
            [(ids_hbm, ids_v), (tab_hbm, tab.at[core]), (gain_hbm, gain_v),
             (rope_t_hbm, rope_t), (rope_s_hbm, rope_s)]
        )
    ]
    for c in loads:
        c.start()
    weights = {}
    for layer in range(LAYERS):
        for i, (a, b) in enumerate([(wk_hbm, wk), (wv_hbm, wv), (wq_hbm, wq), (wo_hbm, wo)]):
            c = pltpu.make_async_copy(a.at[layer], b.at[layer], w_sem.at[layer, i])
            c.start(priority=1)
            weights[layer, i] = c

    loads[0].wait()
    sub = lax.broadcasted_iota(I32, (t_len, t_len), 0)
    lane = lax.broadcasted_iota(I32, (t_len, t_len), 1)
    idr = jnp.broadcast_to(ids_v[...], (t_len, t_len))
    idc = idr.T

    def chip_of(ids):
        return ((ids.astype(F32) + 0.5) * (1.0 / (2 * vr))).astype(I32)

    pr, pc = chip_of(idr), chip_of(idc)
    same = idr == idc
    one = jnp.ones((), I32)
    zero = jnp.zeros((), I32)
    dup_row = jnp.sum(jnp.where(same & (sub < lane), one, zero), axis=0, keepdims=True)
    dup_col = jnp.sum(jnp.where(same & (lane < sub), one, zero), axis=1, keepdims=True)
    first_row, first_col = dup_row == 0, dup_col == 0
    peer = pr == pc
    rank_row = jnp.sum(jnp.where(peer & (idc < idr) & first_col, one, zero), axis=0, keepdims=True)
    rank_col = jnp.sum(jnp.where(peer & (idr < idc) & first_row, one, zero), axis=1, keepdims=True)
    full = jnp.where(jnp.max(rank_row, axis=1, keepdims=True) >= slots, one, zero)
    wanted = jnp.where(first_col, pc[:, 0:1] * t_len + rank_col, -1)
    wanted = jnp.broadcast_to(wanted, (t_len, t_len)) - lane
    local_id = idc - 2 * vr * pc + 1
    lane_row = lane[0:1]
    for slot, dx, dz, _ in offsets:
        row = jnp.where(wanted == chip_at(dx, dz) * t_len, local_id, zero)
        row = jnp.sum(row, axis=0, keepdims=True) - 1
        req_send[slot] = jnp.where(lane_row == t_len - 1, full, row) if slots < t_len else row
    req_recv[0] = req_send[0]

    px = sum(jnp.where(pc >= i * nz, one, zero) for i in range(1, nx)) if nx > 1 else jnp.zeros_like(pc)
    rx, rz = px - x, pc - px * nz - z
    rel = jnp.where(rx < 0, rx + nx, rx) * nz + jnp.where(rz < 0, rz + nz, rz)
    slot_key = rel[:, 0:1] * slots + rank_col
    slots_iota = lax.broadcasted_iota(I32, (t_len, n_chip * slots), 1)
    unpack = jnp.where(jnp.broadcast_to(slot_key, slots_iota.shape) == slots_iota, 1.0, 0.0).astype(BF16)

    @pl.when(s == 0)
    def _():
        kv_past[...] = jnp.zeros_like(kv_past)

    pl.semaphore_wait(bar, 3 + 2 + n_chip - 1)

    group = min(4, n_chip)
    group_of = {o[0]: i // group for i, o in enumerate(offsets)}
    for slot, dx, dz, back in offsets[:0:-1]:
        remote(
            req_send.at[slot], req_recv.at[back], req_s.at[0], req_r.at[group_of[back]],
            2 * chip_at(dx, dz) + core, h,
        ).start()
    tab_copy = remote(tab_hbm, tab.at[core], tab_sem.at[0], tab_sem.at[1], sib, h)
    tab_copy.start()
    loads[1].wait()
    row_iota = lax.broadcasted_iota(I32, (slots, vr), 1)

    pk_copies = {}
    for f, (f0, f1) in enumerate(f_cuts):
        cols = pl.ds(f0, f1 - f0)
        for g in range(n_chip // group):
            members = offsets[g * group:(g + 1) * group]
            rows = pl.ds(g * group * slots, group * slots)
            if f == 0:
                came = req_recv.at[pl.ds(0, sum(o[0] != 0 for o in members))]
                pltpu.make_async_copy(came, came, req_r.at[g]).wait()
                asked = jnp.concatenate(
                    [req_recv[o[0]] for o in members] + [jnp.zeros((t_len - group, t_len), I32)], axis=0
                ).T
                away = jnp.concatenate(
                    [jnp.broadcast_to(asked[:slots, i:i + 1], (slots, vr)) - row_iota for i in range(group)], axis=0
                )
                if g == 0:
                    tab_copy.wait_recv()
                hot[0, rows] = jnp.where(away == 0, 1.0, 0.0).astype(BF16)
                hot[1, rows] = jnp.where(away == vr, 1.0, 0.0).astype(BF16)
            found = dot(hot[0, rows], tab[0, :, cols]) + dot(hot[1, rows], tab[1, :, cols])
            for i, (slot, dx, dz, back) in enumerate(members):
                piece = found[i * slots:(i + 1) * slots].astype(BF16)
                if slot == 0:
                    pk_recv[0, :, cols] = piece
                else:
                    pk_send[slot, :, cols] = piece
                    remote(
                        pk_send.at[slot, :, cols], pk_recv.at[back, :, cols], pk_s.at[f], pk_r.at[f],
                        2 * chip_at(dx, dz) + core, h,
                    ).start()

    reqs = jnp.concatenate([req_recv[p] for p in range(n_chip)], axis=0)
    any_full = jnp.max(reqs, axis=0, keepdims=True)
    any_full = jnp.max(jnp.where(lane_row == t_len - 1, any_full, zero), axis=1, keepdims=True)
    flag_send[...] = jnp.broadcast_to(any_full, (8, t_len))
    flag_copy = remote(flag_send, flag_recv, flag_sem.at[0], flag_sem.at[1], sib, h)
    flag_copy.start()

    for c in loads[2:]:
        c.wait()
    cos_t, sin_t = rope_t[0], rope_t[1]
    cos_s, sin_s = rope_s[0, pl.ds(s, 1), :], rope_s[1, pl.ds(s, 1), :]
    cosine = cos_t * cos_s - sin_t * sin_s
    sine = sin_t * cos_s + cos_t * sin_s
    lane128 = lax.broadcasted_iota(I32, (t_len, 128), 1)
    front = lax.rem(lane128, HD) < HD // 2
    sine = jnp.where(front, -sine, sine)

    def rope(x, scale):
        pieces = []
        for j in range(0, hw, 128):
            y = x[:, j:j + 128] * scale
            partner = jnp.where(front, pltpu.roll(y, 128 - HD // 2, 1), pltpu.roll(y, HD // 2, 1))
            pieces.append(y * cosine + partner * sine)
        return jnp.concatenate(pieces, axis=1)

    causal = lane[:, :t_len] <= sub[:, :t_len]
    causal2 = jnp.concatenate([causal, causal], axis=0)
    head_a = lane128 < HD
    ones = jnp.ones((t_len, 128), BF16)
    sends = []

    def halves(region):
        r0, r1, c0, c1 = region
        mid, cols = (r0 + r1) // 2, pl.ds(c0, c1 - c0)
        return (pl.ds(r0, mid - r0), cols), (pl.ds(mid, r1 - mid), cols)

    def straight(layer, i):
        return layer == 1 and i == 1

    def share(layer, i, region):
        a, b = halves(region)
        own, low, high = st.at[layer, 0], st.at[layer, 1], st.at[layer, 2]

        def both(k, part):
            cu = remote(own.at[part], low.at[part], ag_s.at[layer, i, 0, k], ag_r.at[layer, i, 0, k], s, up)
            cd = remote(own.at[part], high.at[part], ag_s.at[layer, i, 1, k], ag_r.at[layer, i, 1, k], s, dn)
            return cu, cd

        (ua, da), (ub, db) = both(0, a), both(1, b)
        for c in (ua, db, ub, da):
            c.start()
        sends.extend([ua, db, ub, da])
        if straight(layer, i):
            whole = (pl.ds(region[0], region[1] - region[0]), b[1])
            c = remote(
                own.at[whole], st.at[layer, 3].at[whole], agf_s.at[layer, i, 0], agf_r.at[layer, i, 0], s, opp
            )
            c.start()
            sends.append(c)
            return ua, da, ub, db, c
        return ua, da, ub, db

    def pass_on(layer, i, region, copies):
        if straight(layer, i):
            copies[0].wait_recv()
            copies[3].wait_recv()
            return copies[4:]
        ua, da, ub, db = copies
        a, b = halves(region)
        low, high, far = st.at[layer, 1], st.at[layer, 2], st.at[layer, 3]
        fu = remote(low.at[a], far.at[a], agf_s.at[layer, i, 0], agf_r.at[layer, i, 0], s, up)
        fd = remote(high.at[b], far.at[b], agf_s.at[layer, i, 1], agf_r.at[layer, i, 1], s, dn)
        ua.wait_recv()
        fu.start()
        db.wait_recv()
        fd.start()
        sends.extend([fu, fd])
        return fu, fd

    def project(layer, k, c0, c1, first, which=(0, 1, 2)):
        start = blocks[k] * cw + c0
        x = st[layer, k, :, c0:c1].astype(F32)
        rows = pl.ds(pl.multiple_of(start, 128), c1 - c0)
        gain = gain_v[pl.ds(layer, 1), rows]
        xg = (x * gain).astype(BF16)
        for i in which:
            y = dot(xg, (wk, wv, wq)[i][layer, rows, :])
            if first:
                acc[i] = y
            else:
                acc[i] += y
        return jnp.sum(x * x, axis=1, keepdims=True)

    for layer in range(LAYERS):
        last = layer == LAYERS - 1
        if layer == 0:
            regions = [(0, t_len, f0, f1) for f0, f1 in f_cuts]
            copies, passed = [], []
            square = jnp.zeros((t_len, 1), F32)
            for i, region in enumerate(regions):
                cols = pl.ds(region[2], region[3] - region[2])
                came = pk_recv.at[pl.ds(1, n_chip - 1), :, cols]
                pltpu.make_async_copy(came, came, pk_r.at[i]).wait()
                packed = pk_recv[:, :, cols].reshape(n_chip * slots, region[3] - region[2])
                st[0, 0, :, cols] = dot(unpack, packed).astype(BF16)
                copies.append(share(layer, i, region))
                if i == 0:
                    for w in range(3):
                        weights[layer, w].wait()
                square += project(layer, 0, *region[2:], i == 0)
            passed = [pass_on(layer, i, region, copies[i]) for i, region in enumerate(regions)]
            for i, region in enumerate(regions):
                ua, da, ub, db = copies[i][:4]
                ub.wait_recv()
                square += project(layer, 1, *region[2:], False)
                da.wait_recv()
                square += project(layer, 2, *region[2:], False)
                for c in passed[i]:
                    c.wait_recv()
                final = (layer, 3, *region[2:], False)
                square += project(*final, (0, 1) if i == len(regions) - 1 else (0, 1, 2))
        else:
            for w in range(3):
                weights[layer, w].wait()
            square = project(layer, 0, 0, cw, True)
            passed = [pass_on(layer, i, region, copies[i]) for i, region in enumerate(regions)]
            for ua, da, ub, db, *_ in copies:
                ub.wait_recv()
            square += project(layer, 1, 0, cw, False)
            for ua, da, ub, db, *_ in copies:
                da.wait_recv()
            square += project(layer, 2, 0, cw, False)
            for pair in passed:
                for c in pair:
                    c.wait_recv()
            final = (layer, 3, 0, cw, False)
            square += project(*final, (0, 1))
        scale = lax.rsqrt(square * (1.0 / (4 * cw)) + EPSILON)

        kv_copies = [
            remote(kv_own.at[layer, i], kv_past.at[layer, i], kv_s.at[layer, i], kv_r.at[layer, i], nxt, h)
            for i in range(2)
        ]

        def send_on(i):
            @pl.when(s < n_seg - 1)
            def _():
                kv_copies[i].start()

        kv_own[layer, 0] = rope(acc[0], scale).astype(BF16)
        send_on(0)
        kv_own[layer, 1] = (acc[1] * scale).astype(BF16)
        send_on(1)
        project(*final, (2,))
        q_own[...] = (rope(acc[2], scale) * HD ** (-0.5)).astype(BF16)

        def queries_of(j):
            q = q_own[:, j:j + 128]
            none = jnp.zeros_like(q)
            return jnp.concatenate([jnp.where(head_a, q, none), jnp.where(head_a, none, q)], axis=0)

        for i, j in enumerate(range(0, hw, 128)):
            scores = dot_nt(queries_of(j), kv_own[layer, 0, :, j:j + 128])
            scores = jnp.where(causal2, scores, -1e30)
            top = jnp.max(scores, axis=1, keepdims=True)
            e = jnp.exp(scores - top).astype(BF16)
            values = jnp.concatenate([kv_own[layer, 1, :, j:j + 128], ones], axis=1)
            o_part[i] = dot(e, values)
            mx_part[i] = jnp.broadcast_to(top, (2 * t_len, 128))

        @pl.when(s > 0)
        def _():
            kv_copies[0].wait_recv()
            kv_copies[1].wait_recv()

        for i, j in enumerate(range(0, hw, 128)):
            scores = dot_nt(queries_of(j), kv_past[layer, 0, :, j:j + 128])
            scores = jnp.where(s > 0, scores, -1e30)
            old = mx_part[i]
            top = jnp.maximum(old, jnp.max(scores, axis=1, keepdims=True))
            e = jnp.exp(scores - top).astype(BF16)
            keep = jnp.exp(old - top)
            values = jnp.concatenate([kv_past[layer, 1, :, j:j + 128], ones], axis=1)
            o = dot(e, values)
            num = o_part[i, :, :128] * keep + o[:, :128]
            den = o_part[i, :, 128:] * keep + o[:, 128:]
            m = num / den
            mixed[:, j:j + 128] = jnp.where(head_a, m[:t_len], m[t_len:]).astype(BF16)

        weights[layer, 3].wait()
        part, comb, frecv, rrecv = (
            (part1, comb1, frecv1, rrecv1) if last else (part0, comb0, frecv0, rrecv0)
        )
        n_row, n_col = part.shape[1:]
        if last:
            regions = [(0, n_row, 0, n_col // 2), (0, n_row, n_col // 2, n_col)]
        else:
            regions = [(0, n_row // 2, 0, n_col), (n_row // 2, n_row, 0, n_col)]

        def send(i, k, src, dst, to):
            c = remote(src, dst, rs_s.at[layer, i, k], rs_r.at[layer, i, k], s, to)
            c.start()
            sends.append(c)
            return c

        def far(i):
            a, b = halves(regions[i])
            return (
                send(i, 0, part.at[opp].at[a], frecv.at[0].at[a], up),
                send(i, 1, part.at[opp].at[b], frecv.at[1].at[b], dn),
            )

        def near(i):
            a, b = halves(regions[i])
            return (
                send(i, 2, part.at[up].at[b], rrecv.at[0].at[b], up),
                send(i, 3, part.at[dn].at[a], rrecv.at[1].at[a], dn),
            )

        def join(i, f):
            a, b = halves(regions[i])
            f[0].wait_recv()
            comb[(0,) + a] = (part[(up,) + a].astype(F32) + frecv[(0,) + a].astype(F32)).astype(BF16)
            cu = send(i, 4, comb.at[0].at[a], rrecv.at[0].at[a], up)
            f[1].wait_recv()
            comb[(1,) + b] = (part[(dn,) + b].astype(F32) + frecv[(1,) + b].astype(F32)).astype(BF16)
            return cu, send(i, 5, comb.at[1].at[b], rrecv.at[1].at[b], dn)

        if last:
            fars = []
            for b in range(4):
                y = dot(mixed[...], wo[layer, :, b * cw:(b + 1) * cw]).astype(BF16)
                for d in range(4):
                    part[d, :, b * cw:(b + 1) * cw] = y[d * n_row:(d + 1) * n_row]
                if b % 2 == 1:
                    fars.append(far(b // 2))
            nears = [near(0), near(1)]
        else:
            for b in (opp, up, dn, h):
                y = dot(mixed[...], wo[layer, :, pl.ds(pl.multiple_of(b * cw, 128), cw)])
                part[b] = y.astype(BF16)
                if b is opp:
                    fars = [far(0), far(1)]
                if b is dn:
                    nears = [near(0), near(1)]
        joined = [join(i, fars[i]) for i in range(2)]
        copies = []
        for i, region in enumerate(regions):
            for c in nears[i] + joined[i]:
                c.wait_recv()
            r0, r1, c0, c1 = region
            at = (slice(r0, r1), slice(c0, c1))
            total = part[(h,) + at].astype(F32) + rrecv[(0,) + at].astype(F32) + rrecv[(1,) + at].astype(F32)
            if last:
                rows = pl.ds(pl.multiple_of(h * n_row, n_row), n_row)
                if i == 0:
                    for k in range(4):
                        cols = pl.ds(pl.multiple_of(blocks[k] * cw, 128), cw)
                        out_ref[:, cols] = st[layer, k, rows, :].astype(F32)
                out_ref[at] += total
            else:
                st[(layer + 1, 0) + at] = (st[(layer, 0) + at].astype(F32) + total).astype(BF16)
                copies.append(share(layer + 1, i, region))

        @pl.when(s < n_seg - 1)
        def _():
            for c in kv_copies:
                c.wait_send()

    flag_copy.wait()
    flag_ref[0, 0] = jnp.max(jnp.maximum(flag_send[...], flag_recv[...]))
    tab_copy.wait_send()
    others = req_send.at[pl.ds(0, n_chip - 1)]
    pltpu.make_async_copy(others, others, req_s.at[0]).wait()
    for f, (f0, f1) in enumerate(f_cuts):
        others = pk_send.at[pl.ds(1, n_chip - 1), :, pl.ds(f0, f1 - f0)]
        pltpu.make_async_copy(others, others, pk_s.at[f]).wait()
    for c in sends:
        c.wait_send()


def rotary_tables(n_seg, t_len):
    freq = 10000.0 ** (-np.arange(HD // 2, dtype=np.float64) / (HD // 2))
    freq = np.tile(freq, 128 // (HD // 2))[None]
    local = np.arange(t_len, dtype=np.float64)[:, None] * freq
    start = (np.arange(n_seg, dtype=np.float64) * t_len)[:, None] * freq
    both = lambda a: np.stack([np.cos(a), np.sin(a)]).astype(np.float32)
    return both(local), both(start)


def run(slots, n_seg, token_ids, embed_table, norm_gains, query_weight, key_weight, value_weight, out_weight):
    t_len = token_ids.shape[0]
    vr, cw = embed_table.shape
    hw = query_weight.shape[2]
    n_chip = n_seg // 2
    rope_t, rope_s = rotary_tables(n_seg, t_len)
    f_cuts = [(0, 384), (384, cw)] if cw > 384 else [(0, cw)]
    n_cut = max(2, len(f_cuts))
    rows = t_len // 4
    vmem = pltpu.VMEM
    dma = pltpu.SemaphoreType.DMA
    any_spec = pl.BlockSpec(memory_space=pl.ANY)
    vmem_spec = pl.BlockSpec(memory_space=pltpu.VMEM)
    return pl.pallas_call(
        functools.partial(kernel, slots, n_seg, vr, t_len, cw, hw, f_cuts),
        out_shape=(
            jax.ShapeDtypeStruct((rows, 4 * cw), F32),
            jax.ShapeDtypeStruct((1, 1), I32),
        ),
        in_specs=[any_spec] * 9,
        out_specs=(vmem_spec, pl.BlockSpec(memory_space=pltpu.SMEM)),
        scratch_shapes=[
            vmem((1, t_len), I32),
            vmem(norm_gains.shape, F32),
            vmem(rope_t.shape, F32),
            vmem(rope_s.shape, F32),
            vmem((2, vr, cw), BF16),
            vmem(query_weight.shape, BF16),
            vmem(key_weight.shape, BF16),
            vmem(value_weight.shape, BF16),
            vmem(out_weight.shape, BF16),
            vmem((n_chip, 1, t_len), I32),
            vmem((n_chip, 1, t_len), I32),
            vmem((8, t_len), I32),
            vmem((8, t_len), I32),
            vmem((2, n_chip * slots, vr), BF16),
            vmem((n_chip, slots, cw), BF16),
            vmem((n_chip, slots, cw), BF16),
            vmem((LAYERS, 4, t_len, cw), BF16),
            vmem((3, t_len, hw), F32),
            vmem((LAYERS, 2, t_len, hw), BF16),
            vmem((LAYERS, 2, t_len, hw), BF16),
            vmem((t_len, hw), BF16),
            vmem((hw // 128, 2 * t_len, 256), F32),
            vmem((hw // 128, 2 * t_len, 128), F32),
            vmem((t_len, hw), BF16),
            vmem((4, t_len, cw), BF16),
            vmem((4, rows, 4 * cw), BF16),
            vmem((2, t_len, cw), BF16),
            vmem((2, rows, 4 * cw), BF16),
            vmem((2, t_len, cw), BF16),
            vmem((2, rows, 4 * cw), BF16),
            vmem((2, t_len, cw), BF16),
            vmem((2, rows, 4 * cw), BF16),
            dma((5,)),
            dma((LAYERS, 4)),
            dma((2,)),
            dma((1,)),
            dma((n_chip,)),
            dma((2,)),
            dma((n_cut,)),
            dma((n_cut,)),
            dma((LAYERS, n_cut, 2, 2)),
            dma((LAYERS, n_cut, 2, 2)),
            dma((LAYERS, n_cut, 2)),
            dma((LAYERS, n_cut, 2)),
            dma((LAYERS, 2)),
            dma((LAYERS, 2)),
            dma((LAYERS, 2, 6)),
            dma((LAYERS, 2, 6)),
        ],
        compiler_params=pltpu.CompilerParams(
            collective_id=int(slots == ALL_SLOTS), has_side_effects=True, vmem_limit_bytes=56 * 2 ** 20
        ),
        name="decoder",
    )(
        token_ids.reshape(1, t_len), embed_table, norm_gains,
        query_weight, key_weight, value_weight, out_weight,
        jnp.asarray(rope_t), jnp.asarray(rope_s),
    )


def body(n_seg, *arrays):
    out, flag = run(SLOTS, n_seg, *arrays)
    return lax.cond(
        flag[0, 0] > 0,
        lambda: run(ALL_SLOTS, n_seg, *arrays)[0].astype(BF16),
        lambda: out.astype(BF16),
    )


def solution(mesh):
    placed = (
        P("seg"),
        P("seg", "head"),
        P(),
        P(None, None, "head"),
        P(None, None, "head"),
        P(None, None, "head"),
        P(None, "head", None),
    )
    return jax.shard_map(
        functools.partial(body, mesh.shape["seg"]),
        mesh=mesh, in_specs=placed, out_specs=P(("seg", "head"), None), check_vma=False,
    )
```

```python
import functools

import jax
import jax.numpy as jnp
import numpy as np
from jax import lax
from jax.experimental import pallas as pl
from jax.experimental.pallas import tpu as pltpu
from jax.sharding import PartitionSpec as P

HD = 64
LAYERS = 2
EPSILON = 1e-05
SLOTS, ALL_SLOTS = 24, 128
MESH = pl.DeviceIdType.MESH
F32 = jnp.float32
BF16 = jnp.bfloat16
I32 = jnp.int32


def dot(a, b):
    return jnp.dot(a, b, preferred_element_type=F32)


def dot_nt(a, b):
    return lax.dot_general(a, b, (((1,), (1,)), ((), ())), preferred_element_type=F32)


def plane(n_chip):
    nx, nz = (4, n_chip // 4) if n_chip % 4 == 0 else (1, n_chip)
    far = lambda d, n: min(d, n - d)
    slots = [
        (dx * nz + dz, dx, dz, (-dx) % nx * nz + (-dz) % nz) for dx in range(nx) for dz in range(nz)
    ]
    return nx, nz, sorted(slots, key=lambda o: far(o[1], nx) + far(o[2], nz))


def kernel(
    slots, n_seg, vr, t_len, cw, hw, f_cuts,
    ids_hbm, tab_hbm, gain_hbm, wq_hbm, wk_hbm, wv_hbm, wo_hbm, rope_t_hbm, rope_s_hbm,
    out_ref, flag_ref,
    ids_v, gain_v, rope_t, rope_s, tab, wq, wk, wv, wo,
    req_send, req_recv, flag_send, flag_recv, hot, pk_send, pk_recv,
    st, acc, kv_own, kv_past, q_own, o_part, mx_part, mixed,
    part0, part1, frecv0, frecv1, comb0, comb1, rrecv0, rrecv1,
    l_sem, w_sem, tab_sem, req_s, req_r, flag_sem, pk_s, pk_r,
    ag_s, ag_r, agf_s, agf_r, kv_s, kv_r, rs_s, rs_r,
):
    s = lax.axis_index("seg")
    h = lax.axis_index("head")
    chip, core = s // 2, lax.rem(s, 2)
    n_chip = n_seg // 2
    nx, nz, offsets = plane(n_chip)
    x, z = chip // nz, lax.rem(chip, nz)
    up, dn, opp = lax.rem(h + 1, 4), lax.rem(h + 3, 4), lax.rem(h + 2, 4)
    sib = s + 1 - 2 * core
    nxt, prv = lax.rem(s + 1, n_seg), lax.rem(s + n_seg - 1, n_seg)
    blocks = (h, dn, up, opp)

    def chip_at(dx, dz):
        return lax.rem(x + dx, nx) * nz + lax.rem(z + dz, nz)

    def remote(src, dst, ss, rs, seg, head):
        return pltpu.make_async_remote_copy(
            src_ref=src, dst_ref=dst, send_sem=ss, recv_sem=rs,
            device_id=(seg, head), device_id_type=MESH,
        )

    bar = pltpu.get_barrier_semaphore()

    def hello(seg, head):
        pl.semaphore_signal(bar, inc=1, device_id=(seg, head), device_id_type=MESH)

    for _, dx, dz, _ in offsets[:0:-1]:
        hello(2 * chip_at(dx, dz) + core, h)
    for other in (up, dn):
        hello(s, other)
    hello(s, opp)
    hello(sib, h)
    hello(prv, h)

    loads = [
        pltpu.make_async_copy(a, b, l_sem.at[i])
        for i, (a, b) in enumerate(
            [(ids_hbm, ids_v), (tab_hbm, tab.at[core]), (gain_hbm, gain_v),
             (rope_t_hbm, rope_t), (rope_s_hbm, rope_s)]
        )
    ]
    for c in loads:
        c.start()
    weights = {}
    for layer in range(LAYERS):
        for i, (a, b) in enumerate([(wk_hbm, wk), (wv_hbm, wv), (wq_hbm, wq), (wo_hbm, wo)]):
            c = pltpu.make_async_copy(a.at[layer], b.at[layer], w_sem.at[layer, i])
            c.start(priority=1)
            weights[layer, i] = c

    loads[0].wait()
    sub = lax.broadcasted_iota(I32, (t_len, t_len), 0)
    lane = lax.broadcasted_iota(I32, (t_len, t_len), 1)
    idr = jnp.broadcast_to(ids_v[...], (t_len, t_len))
    idc = idr.T

    def chip_of(ids):
        return ((ids.astype(F32) + 0.5) * (1.0 / (2 * vr))).astype(I32)

    pr, pc = chip_of(idr), chip_of(idc)
    same = idr == idc
    one = jnp.ones((), I32)
    zero = jnp.zeros((), I32)
    dup_row = jnp.sum(jnp.where(same & (sub < lane), one, zero), axis=0, keepdims=True)
    dup_col = jnp.sum(jnp.where(same & (lane < sub), one, zero), axis=1, keepdims=True)
    first_row, first_col = dup_row == 0, dup_col == 0
    peer = pr == pc
    rank_row = jnp.sum(jnp.where(peer & (idc < idr) & first_col, one, zero), axis=0, keepdims=True)
    rank_col = jnp.sum(jnp.where(peer & (idr < idc) & first_row, one, zero), axis=1, keepdims=True)
    full = jnp.where(jnp.max(rank_row, axis=1, keepdims=True) >= slots, one, zero)
    wanted = jnp.where(first_col, pc[:, 0:1] * t_len + rank_col, -1)
    wanted = jnp.broadcast_to(wanted, (t_len, t_len)) - lane
    local_id = idc - 2 * vr * pc + 1
    lane_row = lane[0:1]
    for slot, dx, dz, _ in offsets:
        row = jnp.where(wanted == chip_at(dx, dz) * t_len, local_id, zero)
        row = jnp.sum(row, axis=0, keepdims=True) - 1
        req_send[slot] = jnp.where(lane_row == t_len - 1, full, row) if slots < t_len else row
    req_recv[0] = req_send[0]

    @pl.when(s == 0)
    def _():
        kv_past[...] = jnp.zeros_like(kv_past)

    pl.semaphore_wait(bar, 3 + 2 + n_chip - 1)

    group = min(4, n_chip)
    group_of = {o[0]: i // group for i, o in enumerate(offsets)}
    for slot, dx, dz, back in offsets[:0:-1]:
        remote(
            req_send.at[slot], req_recv.at[back], req_s.at[0], req_r.at[group_of[back]],
            2 * chip_at(dx, dz) + core, h,
        ).start()
    tab_copy = remote(tab_hbm, tab.at[core], tab_sem.at[0], tab_sem.at[1], sib, h)
    tab_copy.start()
    loads[1].wait()
    row_iota = lax.broadcasted_iota(I32, (slots, vr), 1)

    pk_copies = {}
    for f, (f0, f1) in enumerate(f_cuts):
        cols = pl.ds(f0, f1 - f0)
        for g in range(n_chip // group):
            members = offsets[g * group:(g + 1) * group]
            rows = pl.ds(g * group * slots, group * slots)
            if f == 0:
                came = req_recv.at[pl.ds(0, sum(o[0] != 0 for o in members))]
                pltpu.make_async_copy(came, came, req_r.at[g]).wait()
                asked = jnp.concatenate(
                    [req_recv[o[0]] for o in members] + [jnp.zeros((t_len - group, t_len), I32)], axis=0
                ).T
                away = jnp.concatenate(
                    [jnp.broadcast_to(asked[:slots, i:i + 1], (slots, vr)) - row_iota for i in range(group)], axis=0
                )
                if g == 0:
                    tab_copy.wait_recv()
                hot[0, rows] = jnp.where(away == 0, 1.0, 0.0).astype(BF16)
                hot[1, rows] = jnp.where(away == vr, 1.0, 0.0).astype(BF16)
            found = dot(hot[0, rows], tab[0, :, cols]) + dot(hot[1, rows], tab[1, :, cols])
            for i, (slot, dx, dz, back) in enumerate(members):
                piece = found[i * slots:(i + 1) * slots].astype(BF16)
                if slot == 0:
                    pk_recv[0, :, cols] = piece
                else:
                    pk_send[slot, :, cols] = piece
                    remote(
                        pk_send.at[slot, :, cols], pk_recv.at[back, :, cols], pk_s.at[f], pk_r.at[f],
                        2 * chip_at(dx, dz) + core, h,
                    ).start()

    reqs = jnp.concatenate([req_recv[p] for p in range(n_chip)], axis=0)
    any_full = jnp.max(reqs, axis=0, keepdims=True)
    any_full = jnp.max(jnp.where(lane_row == t_len - 1, any_full, zero), axis=1, keepdims=True)
    flag_send[...] = jnp.broadcast_to(any_full, (8, t_len))
    flag_copy = remote(flag_send, flag_recv, flag_sem.at[0], flag_sem.at[1], sib, h)
    flag_copy.start()

    px = sum(jnp.where(pc >= i * nz, one, zero) for i in range(1, nx)) if nx > 1 else jnp.zeros_like(pc)
    rx, rz = px - x, pc - px * nz - z
    rel = jnp.where(rx < 0, rx + nx, rx) * nz + jnp.where(rz < 0, rz + nz, rz)
    slot_key = rel[:, 0:1] * slots + rank_col
    slots_iota = lax.broadcasted_iota(I32, (t_len, n_chip * slots), 1)
    unpack = jnp.where(jnp.broadcast_to(slot_key, slots_iota.shape) == slots_iota, 1.0, 0.0).astype(BF16)

    for c in loads[2:]:
        c.wait()
    cos_t, sin_t = rope_t[0], rope_t[1]
    cos_s, sin_s = rope_s[0, pl.ds(s, 1), :], rope_s[1, pl.ds(s, 1), :]
    cosine = cos_t * cos_s - sin_t * sin_s
    sine = sin_t * cos_s + cos_t * sin_s
    lane128 = lax.broadcasted_iota(I32, (t_len, 128), 1)
    front = lax.rem(lane128, HD) < HD // 2
    sine = jnp.where(front, -sine, sine)

    def rope(x, scale):
        pieces = []
        for j in range(0, x.shape[1], 128):
            y = x[:, j:j + 128] * scale
            partner = jnp.where(front, pltpu.roll(y, 128 - HD // 2, 1), pltpu.roll(y, HD // 2, 1))
            pieces.append(y * cosine + partner * sine)
        return jnp.concatenate(pieces, axis=1)

    causal = lane[:, :t_len] <= sub[:, :t_len]
    causal2 = jnp.concatenate([causal, causal], axis=0)
    head_a = lane128 < HD
    ones = jnp.ones((t_len, 128), BF16)
    sends = []

    def halves(region):
        r0, r1, c0, c1 = region
        mid, cols = (r0 + r1) // 2, pl.ds(c0, c1 - c0)
        return (pl.ds(r0, mid - r0), cols), (pl.ds(mid, r1 - mid), cols)

    def straight(layer, i):
        return layer == 1 and i == 1

    def share(layer, i, region):
        a, b = halves(region)
        own, low, high = st.at[layer, 0], st.at[layer, 1], st.at[layer, 2]

        def both(k, part):
            cu = remote(own.at[part], low.at[part], ag_s.at[layer, i, 0, k], ag_r.at[layer, i, 0, k], s, up)
            cd = remote(own.at[part], high.at[part], ag_s.at[layer, i, 1, k], ag_r.at[layer, i, 1, k], s, dn)
            return cu, cd

        (ua, da), (ub, db) = both(0, a), both(1, b)
        for c in (ua, db, ub, da):
            c.start()
        sends.extend([ua, db, ub, da])
        if straight(layer, i):
            whole = (pl.ds(region[0], region[1] - region[0]), b[1])
            c = remote(
                own.at[whole], st.at[layer, 3].at[whole], agf_s.at[layer, i, 0], agf_r.at[layer, i, 0], s, opp
            )
            c.start()
            sends.append(c)
            return ua, da, ub, db, c
        return ua, da, ub, db

    def pass_on(layer, i, region, copies):
        if straight(layer, i):
            copies[0].wait_recv()
            copies[3].wait_recv()
            return copies[4:]
        ua, da, ub, db = copies
        a, b = halves(region)
        low, high, far = st.at[layer, 1], st.at[layer, 2], st.at[layer, 3]
        fu = remote(low.at[a], far.at[a], agf_s.at[layer, i, 0], agf_r.at[layer, i, 0], s, up)
        fd = remote(high.at[b], far.at[b], agf_s.at[layer, i, 1], agf_r.at[layer, i, 1], s, dn)
        ua.wait_recv()
        fu.start()
        db.wait_recv()
        fd.start()
        sends.extend([fu, fd])
        return fu, fd

    def project(layer, k, c0, c1, first, which=(0, 1, 2)):
        start = blocks[k] * cw + c0
        x = st[layer, k, :, c0:c1].astype(F32)
        rows = pl.ds(pl.multiple_of(start, 128), c1 - c0)
        gain = gain_v[pl.ds(layer, 1), rows]
        xg = (x * gain).astype(BF16)
        for i in which:
            y = dot(xg, (wk, wv, wq)[i][layer, rows, :])
            if first:
                acc[i] = y
            else:
                acc[i] += y
        return jnp.sum(x * x, axis=1, keepdims=True)

    for layer in range(LAYERS):
        last = layer == LAYERS - 1
        if layer == 0:
            regions = [(0, t_len, f0, f1) for f0, f1 in f_cuts]
            copies, passed = [], []
            square = jnp.zeros((t_len, 1), F32)
            for i, region in enumerate(regions):
                cols = pl.ds(region[2], region[3] - region[2])
                came = pk_recv.at[pl.ds(1, n_chip - 1), :, cols]
                pltpu.make_async_copy(came, came, pk_r.at[i]).wait()
                packed = pk_recv[:, :, cols].reshape(n_chip * slots, region[3] - region[2])
                st[0, 0, :, cols] = dot(unpack, packed).astype(BF16)
                copies.append(share(layer, i, region))
                if i == 0:
                    for w in range(3):
                        weights[layer, w].wait()
                square += project(layer, 0, *region[2:], i == 0)
            passed = [pass_on(layer, i, region, copies[i]) for i, region in enumerate(regions)]
            for i, region in enumerate(regions):
                ua, da, ub, db = copies[i][:4]
                ub.wait_recv()
                square += project(layer, 1, *region[2:], False)
                da.wait_recv()
                square += project(layer, 2, *region[2:], False)
                for c in passed[i]:
                    c.wait_recv()
                final = (layer, 3, *region[2:], False)
                square += project(*final, (0, 1) if i == len(regions) - 1 else (0, 1, 2))
        else:
            for w in range(3):
                weights[layer, w].wait()
            square = project(layer, 0, 0, cw, True)
            passed = [pass_on(layer, i, region, copies[i]) for i, region in enumerate(regions)]
            for ua, da, ub, db, *_ in copies:
                ub.wait_recv()
            square += project(layer, 1, 0, cw, False)
            for ua, da, ub, db, *_ in copies:
                da.wait_recv()
            square += project(layer, 2, 0, cw, False)
            for pair in passed:
                for c in pair:
                    c.wait_recv()
            final = (layer, 3, 0, cw, False)
            square += project(*final, (0, 1))
        scale = lax.rsqrt(square * (1.0 / (4 * cw)) + EPSILON)

        pairs = max(1, hw // 256)
        kv_copies = [
            remote(
                kv_own.at[layer, pl.ds(i, pairs)], kv_past.at[layer, pl.ds(i, pairs)],
                kv_s.at[layer, i], kv_r.at[layer, i], nxt, h,
            )
            for i in range(0, hw // 128, pairs)
        ]

        def send_on(i):
            @pl.when(s < n_seg - 1)
            def _():
                kv_copies[i].start()

        for i in range(hw // 128):
            cols = slice(i * 128, (i + 1) * 128)
            kv_own[layer, i, 0] = rope(acc[0, :, cols], scale).astype(BF16)
            kv_own[layer, i, 1] = (acc[1, :, cols] * scale).astype(BF16)
            if (i + 1) % pairs == 0:
                send_on(i // pairs)
        project(*final, (2,))
        q_own[...] = (rope(acc[2], scale) * HD ** (-0.5)).astype(BF16)

        def queries_of(j):
            q = q_own[:, j:j + 128]
            none = jnp.zeros_like(q)
            return jnp.concatenate([jnp.where(head_a, q, none), jnp.where(head_a, none, q)], axis=0)

        for i, j in enumerate(range(0, hw, 128)):
            scores = dot_nt(queries_of(j), kv_own[layer, i, 0])
            scores = jnp.where(causal2, scores, -1e30)
            top = jnp.max(scores, axis=1, keepdims=True)
            e = jnp.exp(scores - top).astype(BF16)
            values = jnp.concatenate([kv_own[layer, i, 1], ones], axis=1)
            o_part[i] = dot(e, values)
            mx_part[i] = jnp.broadcast_to(top, (2 * t_len, 128))

        for i, j in enumerate(range(0, hw, 128)):
            if i % pairs == 0:
                pl.when(s > 0)(kv_copies[i // pairs].wait_recv)
            scores = dot_nt(queries_of(j), kv_past[layer, i, 0])
            scores = jnp.where(s > 0, scores, -1e30)
            old = mx_part[i]
            top = jnp.maximum(old, jnp.max(scores, axis=1, keepdims=True))
            e = jnp.exp(scores - top).astype(BF16)
            keep = jnp.exp(old - top)
            values = jnp.concatenate([kv_past[layer, i, 1], ones], axis=1)
            o = dot(e, values)
            num = o_part[i, :, :128] * keep + o[:, :128]
            den = o_part[i, :, 128:] * keep + o[:, 128:]
            m = num / den
            mixed[:, j:j + 128] = jnp.where(head_a, m[:t_len], m[t_len:]).astype(BF16)

        weights[layer, 3].wait()
        part, comb, frecv, rrecv = (
            (part1, comb1, frecv1, rrecv1) if last else (part0, comb0, frecv0, rrecv0)
        )
        n_row, n_col = part.shape[1:]
        if last:
            regions = [(0, n_row, 0, n_col // 2), (0, n_row, n_col // 2, n_col)]
        else:
            regions = [(0, n_row // 2, 0, n_col), (n_row // 2, n_row, 0, n_col)]

        def send(i, k, src, dst, to):
            c = remote(src, dst, rs_s.at[layer, i, k], rs_r.at[layer, i, k], s, to)
            c.start()
            sends.append(c)
            return c

        def far(i):
            a, b = halves(regions[i])
            return (
                send(i, 0, part.at[opp].at[a], frecv.at[0].at[a], up),
                send(i, 1, part.at[opp].at[b], frecv.at[1].at[b], dn),
            )

        def near(i):
            a, b = halves(regions[i])
            return (
                send(i, 2, part.at[up].at[b], rrecv.at[0].at[b], up),
                send(i, 3, part.at[dn].at[a], rrecv.at[1].at[a], dn),
            )

        def join(i, f):
            a, b = halves(regions[i])
            f[0].wait_recv()
            comb[(0,) + a] = (part[(up,) + a].astype(F32) + frecv[(0,) + a].astype(F32)).astype(BF16)
            cu = send(i, 4, comb.at[0].at[a], rrecv.at[0].at[a], up)
            f[1].wait_recv()
            comb[(1,) + b] = (part[(dn,) + b].astype(F32) + frecv[(1,) + b].astype(F32)).astype(BF16)
            return cu, send(i, 5, comb.at[1].at[b], rrecv.at[1].at[b], dn)

        if last:
            fars = []
            for b in range(4):
                y = dot(mixed[...], wo[layer, :, b * cw:(b + 1) * cw]).astype(BF16)
                for d in range(4):
                    part[d, :, b * cw:(b + 1) * cw] = y[d * n_row:(d + 1) * n_row]
                if b % 2 == 1:
                    fars.append(far(b // 2))
            nears = [near(0), near(1)]
        else:
            for b in (opp, up, dn, h):
                y = dot(mixed[...], wo[layer, :, pl.ds(pl.multiple_of(b * cw, 128), cw)])
                part[b] = y.astype(BF16)
                if b is opp:
                    fars = [far(0), far(1)]
                if b is dn:
                    nears = [near(0), near(1)]
        joined = [join(i, fars[i]) for i in range(2)]
        copies = []
        for i, region in enumerate(regions):
            for c in nears[i] + joined[i]:
                c.wait_recv()
            r0, r1, c0, c1 = region
            at = (slice(r0, r1), slice(c0, c1))
            total = part[(h,) + at].astype(F32) + rrecv[(0,) + at].astype(F32) + rrecv[(1,) + at].astype(F32)
            if last:
                rows = pl.ds(pl.multiple_of(h * n_row, n_row), n_row)
                if i == 0:
                    for k in range(4):
                        cols = pl.ds(pl.multiple_of(blocks[k] * cw, 128), cw)
                        out_ref[:, cols] = st[layer, k, rows, :].astype(F32)
                out_ref[at] += total
            else:
                st[(layer + 1, 0) + at] = (st[(layer, 0) + at].astype(F32) + total).astype(BF16)
                copies.append(share(layer + 1, i, region))

        @pl.when(s < n_seg - 1)
        def _():
            for c in kv_copies:
                c.wait_send()

    flag_copy.wait()
    flag_ref[0, 0] = jnp.max(jnp.maximum(flag_send[...], flag_recv[...]))
    tab_copy.wait_send()
    others = req_send.at[pl.ds(0, n_chip - 1)]
    pltpu.make_async_copy(others, others, req_s.at[0]).wait()
    for f, (f0, f1) in enumerate(f_cuts):
        others = pk_send.at[pl.ds(1, n_chip - 1), :, pl.ds(f0, f1 - f0)]
        pltpu.make_async_copy(others, others, pk_s.at[f]).wait()
    for c in sends:
        c.wait_send()


def rotary_tables(n_seg, t_len):
    freq = 10000.0 ** (-np.arange(HD // 2, dtype=np.float64) / (HD // 2))
    freq = np.tile(freq, 128 // (HD // 2))[None]
    local = np.arange(t_len, dtype=np.float64)[:, None] * freq
    start = (np.arange(n_seg, dtype=np.float64) * t_len)[:, None] * freq
    both = lambda a: np.stack([np.cos(a), np.sin(a)]).astype(np.float32)
    return both(local), both(start)


def run(slots, n_seg, token_ids, embed_table, norm_gains, query_weight, key_weight, value_weight, out_weight):
    t_len = token_ids.shape[0]
    vr, cw = embed_table.shape
    hw = query_weight.shape[2]
    n_chip = n_seg // 2
    rope_t, rope_s = rotary_tables(n_seg, t_len)
    f_cuts = [(0, 384), (384, cw)] if cw > 384 else [(0, cw)]
    n_cut = max(2, len(f_cuts))
    rows = t_len // 4
    vmem = pltpu.VMEM
    dma = pltpu.SemaphoreType.DMA
    any_spec = pl.BlockSpec(memory_space=pl.ANY)
    vmem_spec = pl.BlockSpec(memory_space=pltpu.VMEM)
    return pl.pallas_call(
        functools.partial(kernel, slots, n_seg, vr, t_len, cw, hw, f_cuts),
        out_shape=(
            jax.ShapeDtypeStruct((rows, 4 * cw), F32),
            jax.ShapeDtypeStruct((1, 1), I32),
        ),
        in_specs=[any_spec] * 9,
        out_specs=(vmem_spec, pl.BlockSpec(memory_space=pltpu.SMEM)),
        scratch_shapes=[
            vmem((1, t_len), I32),
            vmem(norm_gains.shape, F32),
            vmem(rope_t.shape, F32),
            vmem(rope_s.shape, F32),
            vmem((2, vr, cw), BF16),
            vmem(query_weight.shape, BF16),
            vmem(key_weight.shape, BF16),
            vmem(value_weight.shape, BF16),
            vmem(out_weight.shape, BF16),
            vmem((n_chip, 1, t_len), I32),
            vmem((n_chip, 1, t_len), I32),
            vmem((8, t_len), I32),
            vmem((8, t_len), I32),
            vmem((2, n_chip * slots, vr), BF16),
            vmem((n_chip, slots, cw), BF16),
            vmem((n_chip, slots, cw), BF16),
            vmem((LAYERS, 4, t_len, cw), BF16),
            vmem((3, t_len, hw), F32),
            vmem((LAYERS, hw // 128, 2, t_len, 128), BF16),
            vmem((LAYERS, hw // 128, 2, t_len, 128), BF16),
            vmem((t_len, hw), BF16),
            vmem((hw // 128, 2 * t_len, 256), F32),
            vmem((hw // 128, 2 * t_len, 128), F32),
            vmem((t_len, hw), BF16),
            vmem((4, t_len, cw), BF16),
            vmem((4, rows, 4 * cw), BF16),
            vmem((2, t_len, cw), BF16),
            vmem((2, rows, 4 * cw), BF16),
            vmem((2, t_len, cw), BF16),
            vmem((2, rows, 4 * cw), BF16),
            vmem((2, t_len, cw), BF16),
            vmem((2, rows, 4 * cw), BF16),
            dma((5,)),
            dma((LAYERS, 4)),
            dma((2,)),
            dma((1,)),
            dma((n_chip,)),
            dma((2,)),
            dma((n_cut,)),
            dma((n_cut,)),
            dma((LAYERS, n_cut, 2, 2)),
            dma((LAYERS, n_cut, 2, 2)),
            dma((LAYERS, n_cut, 2)),
            dma((LAYERS, n_cut, 2)),
            dma((LAYERS, hw // 128)),
            dma((LAYERS, hw // 128)),
            dma((LAYERS, 2, 6)),
            dma((LAYERS, 2, 6)),
        ],
        compiler_params=pltpu.CompilerParams(
            collective_id=int(slots == ALL_SLOTS), has_side_effects=True, vmem_limit_bytes=56 * 2 ** 20
        ),
        name="decoder",
    )(
        token_ids.reshape(1, t_len), embed_table, norm_gains,
        query_weight, key_weight, value_weight, out_weight,
        jnp.asarray(rope_t), jnp.asarray(rope_s),
    )


def body(n_seg, *arrays):
    out, flag = run(SLOTS, n_seg, *arrays)
    return lax.cond(
        flag[0, 0] > 0,
        lambda: run(ALL_SLOTS, n_seg, *arrays)[0].astype(BF16),
        lambda: out.astype(BF16),
    )


def solution(mesh):
    placed = (
        P("seg"),
        P("seg", "head"),
        P(),
        P(None, None, "head"),
        P(None, None, "head"),
        P(None, None, "head"),
        P(None, "head", None),
    )
    return jax.shard_map(
        functools.partial(body, mesh.shape["seg"]),
        mesh=mesh, in_specs=placed, out_specs=P(("seg", "head"), None), check_vma=False,
    )
```

```python
import functools

import jax
import jax.numpy as jnp
import numpy as np
from jax import lax
from jax.experimental import pallas as pl
from jax.experimental.pallas import tpu as pltpu
from jax.sharding import PartitionSpec as P

HD = 64
LAYERS = 2
EPSILON = 1e-05
SLOTS, ALL_SLOTS = 24, 128
MESH = pl.DeviceIdType.MESH
F32 = jnp.float32
BF16 = jnp.bfloat16
I32 = jnp.int32


def dot(a, b):
    return jnp.dot(a, b, preferred_element_type=F32)


def dot_nt(a, b):
    return lax.dot_general(a, b, (((1,), (1,)), ((), ())), preferred_element_type=F32)


def plane(n_chip):
    nx, nz = (4, n_chip // 4) if n_chip % 4 == 0 else (1, n_chip)
    far = lambda d, n: min(d, n - d)
    slots = [
        (dx * nz + dz, dx, dz, (-dx) % nx * nz + (-dz) % nz) for dx in range(nx) for dz in range(nz)
    ]
    return nx, nz, sorted(slots, key=lambda o: far(o[1], nx) + far(o[2], nz))


def kernel(
    slots, n_seg, vr, t_len, cw, hw, f_cuts,
    ids_hbm, tab_hbm, gain_hbm, wq_hbm, wk_hbm, wv_hbm, wo_hbm, rope_t_hbm, rope_s_hbm,
    out_ref, flag_ref,
    ids_v, gain_v, rope_t, rope_s, tab, wq, wk, wv, wo,
    req_send, req_recv, flag_send, flag_recv, hot, pk_send, pk_recv,
    st, acc, kv_own, kv_past, q_own, o_part, mx_part, mixed,
    part0, part1, frecv0, frecv1, comb0, comb1, rrecv0, rrecv1,
    l_sem, w_sem, tab_sem, req_s, req_r, flag_sem, pk_s, pk_r,
    ag_s, ag_r, agf_s, agf_r, kv_s, kv_r, rs_s, rs_r,
):
    s = lax.axis_index("seg")
    h = lax.axis_index("head")
    chip, core = s // 2, lax.rem(s, 2)
    n_chip = n_seg // 2
    nx, nz, offsets = plane(n_chip)
    x, z = chip // nz, lax.rem(chip, nz)
    up, dn, opp = lax.rem(h + 1, 4), lax.rem(h + 3, 4), lax.rem(h + 2, 4)
    sib = s + 1 - 2 * core
    nxt, prv = lax.rem(s + 1, n_seg), lax.rem(s + n_seg - 1, n_seg)
    blocks = (h, dn, up, opp)

    def chip_at(dx, dz):
        return lax.rem(x + dx, nx) * nz + lax.rem(z + dz, nz)

    def remote(src, dst, ss, rs, seg, head):
        return pltpu.make_async_remote_copy(
            src_ref=src, dst_ref=dst, send_sem=ss, recv_sem=rs,
            device_id=(seg, head), device_id_type=MESH,
        )

    bar = pltpu.get_barrier_semaphore()

    def hello(seg, head):
        pl.semaphore_signal(bar, inc=1, device_id=(seg, head), device_id_type=MESH)

    for _, dx, dz, _ in offsets[:0:-1]:
        hello(2 * chip_at(dx, dz) + core, h)
    for other in (up, dn):
        hello(s, other)
    hello(s, opp)
    hello(sib, h)
    hello(prv, h)

    loads = [
        pltpu.make_async_copy(a, b, l_sem.at[i])
        for i, (a, b) in enumerate(
            [(ids_hbm, ids_v), (tab_hbm, tab.at[core]), (gain_hbm, gain_v),
             (rope_t_hbm, rope_t), (rope_s_hbm, rope_s)]
        )
    ]
    for c in loads:
        c.start()
    weights = {}
    for layer in range(LAYERS):
        for i, (a, b) in enumerate([(wk_hbm, wk), (wv_hbm, wv), (wq_hbm, wq), (wo_hbm, wo)]):
            c = pltpu.make_async_copy(a.at[layer], b.at[layer], w_sem.at[layer, i])
            c.start(priority=1)
            weights[layer, i] = c

    loads[0].wait()
    sub = lax.broadcasted_iota(I32, (t_len, t_len), 0)
    lane = lax.broadcasted_iota(I32, (t_len, t_len), 1)
    idr = jnp.broadcast_to(ids_v[...], (t_len, t_len))
    idc = idr.T

    def chip_of(ids):
        return ((ids.astype(F32) + 0.5) * (1.0 / (2 * vr))).astype(I32)

    pr, pc = chip_of(idr), chip_of(idc)
    same = idr == idc
    one = jnp.ones((), I32)
    zero = jnp.zeros((), I32)
    dup_row = jnp.sum(jnp.where(same & (sub < lane), one, zero), axis=0, keepdims=True)
    dup_col = jnp.sum(jnp.where(same & (lane < sub), one, zero), axis=1, keepdims=True)
    first_row, first_col = dup_row == 0, dup_col == 0
    peer = pr == pc
    rank_row = jnp.sum(jnp.where(peer & (idc < idr) & first_col, one, zero), axis=0, keepdims=True)
    rank_col = jnp.sum(jnp.where(peer & (idr < idc) & first_row, one, zero), axis=1, keepdims=True)
    full = jnp.where(jnp.max(rank_row, axis=1, keepdims=True) >= slots, one, zero)
    wanted = jnp.where(first_col, pc[:, 0:1] * t_len + rank_col, -1)
    wanted = jnp.broadcast_to(wanted, (t_len, t_len)) - lane
    local_id = idc - 2 * vr * pc + 1
    lane_row = lane[0:1]
    for slot, dx, dz, _ in offsets:
        row = jnp.where(wanted == chip_at(dx, dz) * t_len, local_id, zero)
        row = jnp.sum(row, axis=0, keepdims=True) - 1
        req_send[slot] = jnp.where(lane_row == t_len - 1, full, row) if slots < t_len else row
    req_recv[0] = req_send[0]

    @pl.when(s == 0)
    def _():
        kv_past[...] = jnp.zeros_like(kv_past)

    pl.semaphore_wait(bar, 3 + 2 + n_chip - 1)

    group = min(4, n_chip)
    group_of = {o[0]: i // group for i, o in enumerate(offsets)}
    for slot, dx, dz, back in offsets[:0:-1]:
        remote(
            req_send.at[slot], req_recv.at[back], req_s.at[0], req_r.at[group_of[back]],
            2 * chip_at(dx, dz) + core, h,
        ).start()
    tab_copy = remote(tab_hbm, tab.at[core], tab_sem.at[0], tab_sem.at[1], sib, h)
    tab_copy.start()
    loads[1].wait()
    row_iota = lax.broadcasted_iota(I32, (slots, vr), 1)

    pk_copies = {}
    for f, (f0, f1) in enumerate(f_cuts):
        cols = pl.ds(f0, f1 - f0)
        for g in range(n_chip // group):
            members = offsets[g * group:(g + 1) * group]
            rows = pl.ds(g * group * slots, group * slots)
            if f == 0:
                came = req_recv.at[pl.ds(0, sum(o[0] != 0 for o in members))]
                pltpu.make_async_copy(came, came, req_r.at[g]).wait()
                asked = jnp.concatenate(
                    [req_recv[o[0]] for o in members] + [jnp.zeros((t_len - group, t_len), I32)], axis=0
                ).T
                away = jnp.concatenate(
                    [jnp.broadcast_to(asked[:slots, i:i + 1], (slots, vr)) - row_iota for i in range(group)], axis=0
                )
                if g == 0:
                    tab_copy.wait_recv()
                hot[0, rows] = jnp.where(away == 0, 1.0, 0.0).astype(BF16)
                hot[1, rows] = jnp.where(away == vr, 1.0, 0.0).astype(BF16)
            found = dot(hot[0, rows], tab[0, :, cols]) + dot(hot[1, rows], tab[1, :, cols])
            for i, (slot, dx, dz, back) in enumerate(members):
                piece = found[i * slots:(i + 1) * slots].astype(BF16)
                if slot == 0:
                    pk_recv[0, :, cols] = piece
                else:
                    pk_send[slot, :, cols] = piece
                    remote(
                        pk_send.at[slot, :, cols], pk_recv.at[back, :, cols], pk_s.at[f], pk_r.at[f],
                        2 * chip_at(dx, dz) + core, h,
                    ).start()

    reqs = jnp.concatenate([req_recv[p] for p in range(n_chip)], axis=0)
    any_full = jnp.max(reqs, axis=0, keepdims=True)
    any_full = jnp.max(jnp.where(lane_row == t_len - 1, any_full, zero), axis=1, keepdims=True)
    flag_send[...] = jnp.broadcast_to(any_full, (8, t_len))
    flag_copy = remote(flag_send, flag_recv, flag_sem.at[0], flag_sem.at[1], sib, h)
    flag_copy.start()

    px = sum(jnp.where(pc >= i * nz, one, zero) for i in range(1, nx)) if nx > 1 else jnp.zeros_like(pc)
    rx, rz = px - x, pc - px * nz - z
    rel = jnp.where(rx < 0, rx + nx, rx) * nz + jnp.where(rz < 0, rz + nz, rz)
    slot_key = rel[:, 0:1] * slots + rank_col
    slots_iota = lax.broadcasted_iota(I32, (t_len, n_chip * slots), 1)
    unpack = jnp.where(jnp.broadcast_to(slot_key, slots_iota.shape) == slots_iota, 1.0, 0.0).astype(BF16)

    for c in loads[2:]:
        c.wait()
    cos_t, sin_t = rope_t[0], rope_t[1]
    cos_s, sin_s = rope_s[0, pl.ds(s, 1), :], rope_s[1, pl.ds(s, 1), :]
    cosine = cos_t * cos_s - sin_t * sin_s
    sine = sin_t * cos_s + cos_t * sin_s
    lane128 = lax.broadcasted_iota(I32, (t_len, 128), 1)
    front = lax.rem(lane128, HD) < HD // 2
    sine = jnp.where(front, -sine, sine)

    def rope(x, scale):
        pieces = []
        for j in range(0, x.shape[1], 128):
            y = x[:, j:j + 128] * scale
            partner = jnp.where(front, pltpu.roll(y, 128 - HD // 2, 1), pltpu.roll(y, HD // 2, 1))
            pieces.append(y * cosine + partner * sine)
        return jnp.concatenate(pieces, axis=1)

    causal = lane[:, :t_len] <= sub[:, :t_len]
    causal2 = jnp.concatenate([causal, causal], axis=0)
    head_a = lane128 < HD
    ones = jnp.ones((t_len, 128), BF16)
    sends = []

    def halves(region):
        r0, r1, c0, c1 = region
        mid, cols = (r0 + r1) // 2, pl.ds(c0, c1 - c0)
        return (pl.ds(r0, mid - r0), cols), (pl.ds(mid, r1 - mid), cols)

    def straight(layer, i):
        return layer == 1 and i == 1

    def share(layer, i, region):
        a, b = halves(region)
        own, low, high = st.at[layer, 0], st.at[layer, 1], st.at[layer, 2]

        def both(k, part):
            cu = remote(own.at[part], low.at[part], ag_s.at[layer, i, 0, k], ag_r.at[layer, i, 0, k], s, up)
            cd = remote(own.at[part], high.at[part], ag_s.at[layer, i, 1, k], ag_r.at[layer, i, 1, k], s, dn)
            return cu, cd

        (ua, da), (ub, db) = both(0, a), both(1, b)
        for c in (ua, db, ub, da):
            c.start()
        sends.extend([ua, db, ub, da])
        if straight(layer, i):
            whole = (pl.ds(region[0], region[1] - region[0]), b[1])
            c = remote(
                own.at[whole], st.at[layer, 3].at[whole], agf_s.at[layer, i, 0], agf_r.at[layer, i, 0], s, opp
            )
            c.start()
            sends.append(c)
            return ua, da, ub, db, c
        return ua, da, ub, db

    def pass_on(layer, i, region, copies):
        if straight(layer, i):
            copies[0].wait_recv()
            copies[3].wait_recv()
            return copies[4:]
        ua, da, ub, db = copies
        a, b = halves(region)
        low, high, far = st.at[layer, 1], st.at[layer, 2], st.at[layer, 3]
        fu = remote(low.at[a], far.at[a], agf_s.at[layer, i, 0], agf_r.at[layer, i, 0], s, up)
        fd = remote(high.at[b], far.at[b], agf_s.at[layer, i, 1], agf_r.at[layer, i, 1], s, dn)
        ua.wait_recv()
        fu.start()
        db.wait_recv()
        fd.start()
        sends.extend([fu, fd])
        return fu, fd

    def project(layer, k, c0, c1, first, which=(0, 1, 2)):
        start = blocks[k] * cw + c0
        x = st[layer, k, :, c0:c1].astype(F32)
        rows = pl.ds(pl.multiple_of(start, 128), c1 - c0)
        gain = gain_v[pl.ds(layer, 1), rows]
        xg = (x * gain).astype(BF16)
        for i in which:
            y = dot(xg, (wk, wv, wq)[i][layer, rows, :])
            if first:
                acc[i] = y
            else:
                acc[i] += y
        return jnp.sum(x * x, axis=1, keepdims=True)

    for layer in range(LAYERS):
        last = layer == LAYERS - 1
        if layer == 0:
            regions = [(0, t_len, f0, f1) for f0, f1 in f_cuts]
            copies, passed = [], []
            square = jnp.zeros((t_len, 1), F32)
            for i, region in enumerate(regions):
                cols = pl.ds(region[2], region[3] - region[2])
                came = pk_recv.at[pl.ds(1, n_chip - 1), :, cols]
                pltpu.make_async_copy(came, came, pk_r.at[i]).wait()
                packed = pk_recv[:, :, cols].reshape(n_chip * slots, region[3] - region[2])
                st[0, 0, :, cols] = dot(unpack, packed).astype(BF16)
                copies.append(share(layer, i, region))
                if i == 0:
                    for w in range(3):
                        weights[layer, w].wait()
                square += project(layer, 0, *region[2:], i == 0)
            passed = [pass_on(layer, i, region, copies[i]) for i, region in enumerate(regions)]
            for i, region in enumerate(regions):
                ua, da, ub, db = copies[i][:4]
                ub.wait_recv()
                square += project(layer, 1, *region[2:], False)
                da.wait_recv()
                square += project(layer, 2, *region[2:], False)
                for c in passed[i]:
                    c.wait_recv()
                final = (layer, 3, *region[2:], False)
                square += project(*final, (0, 1) if i == len(regions) - 1 else (0, 1, 2))
        else:
            for w in range(3):
                weights[layer, w].wait()
            square = project(layer, 0, 0, cw, True)
            passed = [pass_on(layer, i, region, copies[i]) for i, region in enumerate(regions)]
            for ua, da, ub, db, *_ in copies:
                ub.wait_recv()
            square += project(layer, 1, 0, cw, False)
            for ua, da, ub, db, *_ in copies:
                da.wait_recv()
            square += project(layer, 2, 0, cw, False)
            for pair in passed:
                for c in pair:
                    c.wait_recv()
            final = (layer, 3, 0, cw, False)
            square += project(*final, (0, 1))
        scale = lax.rsqrt(square * (1.0 / (4 * cw)) + EPSILON)

        pairs = max(1, hw // 256)
        kv_copies = [
            remote(
                kv_own.at[layer, pl.ds(i, pairs)], kv_past.at[layer, pl.ds(i, pairs)],
                kv_s.at[layer, i], kv_r.at[layer, i], nxt, h,
            )
            for i in range(0, hw // 128, pairs)
        ]

        def send_on(i):
            @pl.when(s < n_seg - 1)
            def _():
                kv_copies[i].start()

        for i in range(hw // 128):
            cols = slice(i * 128, (i + 1) * 128)
            kv_own[layer, i, 0] = rope(acc[0, :, cols], scale).astype(BF16)
            kv_own[layer, i, 1] = (acc[1, :, cols] * scale).astype(BF16)
            if (i + 1) % pairs == 0:
                send_on(i // pairs)
        project(*final, (2,))
        q_own[...] = (rope(acc[2], scale) * HD ** (-0.5)).astype(BF16)

        def queries_of(j):
            q = q_own[:, j:j + 128]
            none = jnp.zeros_like(q)
            return jnp.concatenate([jnp.where(head_a, q, none), jnp.where(head_a, none, q)], axis=0)

        for i, j in enumerate(range(0, hw, 128)):
            scores = dot_nt(queries_of(j), kv_own[layer, i, 0])
            scores = jnp.where(causal2, scores, -1e30)
            top = jnp.max(scores, axis=1, keepdims=True)
            e = jnp.exp(scores - top).astype(BF16)
            values = jnp.concatenate([kv_own[layer, i, 1], ones], axis=1)
            o_part[i] = dot(e, values)
            mx_part[i] = jnp.broadcast_to(top, (2 * t_len, 128))

        for i, j in enumerate(range(0, hw, 128)):
            if i % pairs == 0:
                pl.when(s > 0)(kv_copies[i // pairs].wait_recv)
            scores = dot_nt(queries_of(j), kv_past[layer, i, 0])
            scores = jnp.where(s > 0, scores, -1e30)
            old = mx_part[i]
            top = jnp.maximum(old, jnp.max(scores, axis=1, keepdims=True))
            e = jnp.exp(scores - top).astype(BF16)
            keep = jnp.exp(old - top)
            values = jnp.concatenate([kv_past[layer, i, 1], ones], axis=1)
            o = dot(e, values)
            num = o_part[i, :, :128] * keep + o[:, :128]
            den = o_part[i, :, 128:] * keep + o[:, 128:]
            m = num / den
            mixed[:, j:j + 128] = jnp.where(head_a, m[:t_len], m[t_len:]).astype(BF16)

        weights[layer, 3].wait()
        part, comb, frecv, rrecv = (
            (part1, comb1, frecv1, rrecv1) if last else (part0, comb0, frecv0, rrecv0)
        )
        n_row, n_col = part.shape[1:]
        if last:
            regions = [(0, n_row, 0, n_col // 2), (0, n_row, n_col // 2, n_col)]
        else:
            regions = [(0, n_row // 2, 0, n_col), (n_row // 2, n_row, 0, n_col)]

        def send(i, k, src, dst, to):
            c = remote(src, dst, rs_s.at[layer, i, k], rs_r.at[layer, i, k], s, to)
            c.start()
            sends.append(c)
            return c

        def far(i):
            a, b = halves(regions[i])
            return (
                send(i, 0, part.at[opp].at[a], frecv.at[0].at[a], up),
                send(i, 1, part.at[opp].at[b], frecv.at[1].at[b], dn),
            )

        def near(i):
            a, b = halves(regions[i])
            return (
                send(i, 2, part.at[up].at[b], rrecv.at[0].at[b], up),
                send(i, 3, part.at[dn].at[a], rrecv.at[1].at[a], dn),
            )

        def join(i, f):
            a, b = halves(regions[i])
            f[0].wait_recv()
            comb[(0,) + a] = part[(up,) + a] + frecv[(0,) + a]
            cu = send(i, 4, comb.at[0].at[a], rrecv.at[0].at[a], up)
            f[1].wait_recv()
            comb[(1,) + b] = part[(dn,) + b] + frecv[(1,) + b]
            return cu, send(i, 5, comb.at[1].at[b], rrecv.at[1].at[b], dn)

        if last:
            fars = []
            for b in range(4):
                y = dot(mixed[...], wo[layer, :, b * cw:(b + 1) * cw]).astype(BF16)
                for d in range(4):
                    part[d, :, b * cw:(b + 1) * cw] = y[d * n_row:(d + 1) * n_row]
                if b % 2 == 1:
                    fars.append(far(b // 2))
            nears = [near(0), near(1)]
        else:
            for b in (opp, up, dn, h):
                y = dot(mixed[...], wo[layer, :, pl.ds(pl.multiple_of(b * cw, 128), cw)])
                part[b] = y.astype(BF16)
                if b is opp:
                    fars = [far(0), far(1)]
                if b is dn:
                    nears = [near(0), near(1)]
        joined = [join(i, fars[i]) for i in range(2)]
        copies = []
        for i, region in enumerate(regions):
            for c in nears[i] + joined[i]:
                c.wait_recv()
            r0, r1, c0, c1 = region
            at = (slice(r0, r1), slice(c0, c1))
            total = part[(h,) + at].astype(F32) + rrecv[(0,) + at].astype(F32) + rrecv[(1,) + at].astype(F32)
            if last:
                rows = pl.ds(pl.multiple_of(h * n_row, n_row), n_row)
                if i == 0:
                    for k in range(4):
                        cols = pl.ds(pl.multiple_of(blocks[k] * cw, 128), cw)
                        out_ref[:, cols] = st[layer, k, rows, :].astype(F32)
                out_ref[at] += total
            else:
                st[(layer + 1, 0) + at] = (st[(layer, 0) + at].astype(F32) + total).astype(BF16)
                copies.append(share(layer + 1, i, region))

        @pl.when(s < n_seg - 1)
        def _():
            for c in kv_copies:
                c.wait_send()

    flag_copy.wait()
    flag_ref[0, 0] = jnp.max(jnp.maximum(flag_send[...], flag_recv[...]))
    tab_copy.wait_send()
    others = req_send.at[pl.ds(0, n_chip - 1)]
    pltpu.make_async_copy(others, others, req_s.at[0]).wait()
    for f, (f0, f1) in enumerate(f_cuts):
        others = pk_send.at[pl.ds(1, n_chip - 1), :, pl.ds(f0, f1 - f0)]
        pltpu.make_async_copy(others, others, pk_s.at[f]).wait()
    for c in sends:
        c.wait_send()


def rotary_tables(n_seg, t_len):
    freq = 10000.0 ** (-np.arange(HD // 2, dtype=np.float64) / (HD // 2))
    freq = np.tile(freq, 128 // (HD // 2))[None]
    local = np.arange(t_len, dtype=np.float64)[:, None] * freq
    start = (np.arange(n_seg, dtype=np.float64) * t_len)[:, None] * freq
    both = lambda a: np.stack([np.cos(a), np.sin(a)]).astype(np.float32)
    return both(local), both(start)


def run(slots, n_seg, token_ids, embed_table, norm_gains, query_weight, key_weight, value_weight, out_weight):
    t_len = token_ids.shape[0]
    vr, cw = embed_table.shape
    hw = query_weight.shape[2]
    n_chip = n_seg // 2
    rope_t, rope_s = rotary_tables(n_seg, t_len)
    f_cuts = [(0, 384), (384, cw)] if cw > 384 else [(0, cw)]
    n_cut = max(2, len(f_cuts))
    rows = t_len // 4
    vmem = pltpu.VMEM
    dma = pltpu.SemaphoreType.DMA
    any_spec = pl.BlockSpec(memory_space=pl.ANY)
    vmem_spec = pl.BlockSpec(memory_space=pltpu.VMEM)
    return pl.pallas_call(
        functools.partial(kernel, slots, n_seg, vr, t_len, cw, hw, f_cuts),
        out_shape=(
            jax.ShapeDtypeStruct((rows, 4 * cw), F32),
            jax.ShapeDtypeStruct((1, 1), I32),
        ),
        in_specs=[any_spec] * 9,
        out_specs=(vmem_spec, pl.BlockSpec(memory_space=pltpu.SMEM)),
        scratch_shapes=[
            vmem((1, t_len), I32),
            vmem(norm_gains.shape, F32),
            vmem(rope_t.shape, F32),
            vmem(rope_s.shape, F32),
            vmem((2, vr, cw), BF16),
            vmem(query_weight.shape, BF16),
            vmem(key_weight.shape, BF16),
            vmem(value_weight.shape, BF16),
            vmem(out_weight.shape, BF16),
            vmem((n_chip, 1, t_len), I32),
            vmem((n_chip, 1, t_len), I32),
            vmem((8, t_len), I32),
            vmem((8, t_len), I32),
            vmem((2, n_chip * slots, vr), BF16),
            vmem((n_chip, slots, cw), BF16),
            vmem((n_chip, slots, cw), BF16),
            vmem((LAYERS, 4, t_len, cw), BF16),
            vmem((3, t_len, hw), F32),
            vmem((LAYERS, hw // 128, 2, t_len, 128), BF16),
            vmem((LAYERS, hw // 128, 2, t_len, 128), BF16),
            vmem((t_len, hw), BF16),
            vmem((hw // 128, 2 * t_len, 256), F32),
            vmem((hw // 128, 2 * t_len, 128), F32),
            vmem((t_len, hw), BF16),
            vmem((4, t_len, cw), BF16),
            vmem((4, rows, 4 * cw), BF16),
            vmem((2, t_len, cw), BF16),
            vmem((2, rows, 4 * cw), BF16),
            vmem((2, t_len, cw), BF16),
            vmem((2, rows, 4 * cw), BF16),
            vmem((2, t_len, cw), BF16),
            vmem((2, rows, 4 * cw), BF16),
            dma((5,)),
            dma((LAYERS, 4)),
            dma((2,)),
            dma((1,)),
            dma((n_chip,)),
            dma((2,)),
            dma((n_cut,)),
            dma((n_cut,)),
            dma((LAYERS, n_cut, 2, 2)),
            dma((LAYERS, n_cut, 2, 2)),
            dma((LAYERS, n_cut, 2)),
            dma((LAYERS, n_cut, 2)),
            dma((LAYERS, hw // 128)),
            dma((LAYERS, hw // 128)),
            dma((LAYERS, 2, 6)),
            dma((LAYERS, 2, 6)),
        ],
        compiler_params=pltpu.CompilerParams(
            collective_id=int(slots == ALL_SLOTS), has_side_effects=True, vmem_limit_bytes=56 * 2 ** 20
        ),
        name="decoder",
    )(
        token_ids.reshape(1, t_len), embed_table, norm_gains,
        query_weight, key_weight, value_weight, out_weight,
        jnp.asarray(rope_t), jnp.asarray(rope_s),
    )


def body(n_seg, *arrays):
    out, flag = run(SLOTS, n_seg, *arrays)
    return lax.cond(
        flag[0, 0] > 0,
        lambda: run(ALL_SLOTS, n_seg, *arrays)[0].astype(BF16),
        lambda: out.astype(BF16),
    )


def solution(mesh):
    placed = (
        P("seg"),
        P("seg", "head"),
        P(),
        P(None, None, "head"),
        P(None, None, "head"),
        P(None, None, "head"),
        P(None, "head", None),
    )
    return jax.shard_map(
        functools.partial(body, mesh.shape["seg"]),
        mesh=mesh, in_specs=placed, out_specs=P(("seg", "head"), None), check_vma=False,
    )
```
